32 devices in a mesh: groups: 2 (over x), tm: 16 (over z, y, core).
Axes of the slice: x: 2, y: 2, z: 4, core: 2. Of those that a mesh axis runs over, the one named last changes fastest.
Arguments:
- queries: bfloat16 [16384, 2560], P(('groups', 'tm')), parts along dimension 0, may hold values from -40 to 40, as said below
- keys: bfloat16 [16384, 2560], P(('groups', 'tm')), parts along dimension 0, may hold values from -48 to 48, as said below
- values: bfloat16 [16384, 2560], P(('groups', 'tm')), parts along dimension 0, may hold values from -8 to 8, as said below
- block_lists: int32 [256, 20, 8], P(('groups', 'tm')), parts along dimension 0, may hold values from 0 to 127, as said below
- gate_coarse: float32 [20], replicated, may hold values from 0.5 to 2
- gate_fine: float32 [20], replicated, may hold values from 0.5 to 2
Outputs:
- blended: bfloat16 [16384, 2560], P(('groups', 'tm')), parts along dimension 0
The draws below stay inside these ranges and needn't reach their ends.
There are 2 independent parts, one for each index of `groups`. The reference program is written for one: setup_inputs(seed, part) draws one part's arguments, and reference() takes and returns one part's arrays. A program takes and returns all parts, laid end to end along the dimension named above; an argument that names none is the same for every part. Nothing has to cross between parts.
Inputs may be any that keep to these rules, and one draw needn't show every extreme that they name: `queries`: queries of the clip; values stay within the range. `keys`: keys of the clip; values stay within the range. `values`: values of the clip; entries stay within the range. `block_lists`: let device j of tm hold cubes 8 * j to 8 * j + 7. The entries of one row (cube, head) name distinct cubes. Over all rows of the cubes of device j, exactly 30 entries name cubes of other devices, at most one in a row; all other entries name cubes of device j. Those 30 entries name the cubes of any one other device at most 4 times, and in every draw one device is named exactly 4 times by the rows of each other device.
All inputs are finite; a program needn't handle non-finite values.
Results may differ from the reference program's by a relative error of at most 0.013.
Values may be sent and summed in bfloat16 or wider, within the bound.
No kernel may reach another device: no remote copies, remote signals or barrier semaphores. Data moves between devices by JAX's collectives and lax.ppermute only.
A program may use at most 128 MiB of HBM per device.

```python
import math
import jax
import jax.numpy as jnp
from jax import lax

HEADS = 20
HEAD_DIM = 128
CUBE = 64
K_TOP = 8
CAP = 4
CUBES_DEV = 8
NC = 128
NTOK = 8192
REMOTE = 30
N_TM = 16


def draw_queries(key, part):
    key = jax.random.fold_in(key, 1)
    subkeys = jax.random.split(key, 2)
    feature_width = HEADS * HEAD_DIM
    common = jax.random.normal(subkeys[0], (NC, 1, feature_width), jnp.float32)
    tokenwise = jax.random.normal(subkeys[1], (NC, CUBE, feature_width), jnp.float32)
    field = common + tokenwise
    return jnp.clip(field, -40.0, 40.0).reshape(NTOK, feature_width).astype(jnp.bfloat16)


def draw_keys(key, part):
    key = jax.random.fold_in(key, 2)
    subkeys = jax.random.split(key, 2)
    feature_width = HEADS * HEAD_DIM
    common = jax.random.normal(subkeys[0], (NC, 1, feature_width), jnp.float32)
    tokenwise = jax.random.normal(subkeys[1], (NC, CUBE, feature_width), jnp.float32)
    field = common + tokenwise
    return jnp.clip(field, -48.0, 48.0).reshape(NTOK, feature_width).astype(jnp.bfloat16)


def draw_values(key, part):
    key = jax.random.fold_in(key, 3)
    subkeys = jax.random.split(key, 2)
    feature_width = HEADS * HEAD_DIM
    common = jax.random.normal(subkeys[0], (NC, 1, feature_width), jnp.float32)
    tokenwise = jax.random.normal(subkeys[1], (NC, CUBE, feature_width), jnp.float32)
    field = common + tokenwise
    return jnp.clip(field, -8.0, 8.0).reshape(NTOK, feature_width).astype(jnp.bfloat16)


def draw_block_lists(key, part):
    key = jax.random.fold_in(key, 4)
    full_key, device_key = jax.random.split(key)
    full_owner = jax.random.randint(full_key, (), 0, N_TM, jnp.int32)
    device_ids = jnp.arange(N_TM, dtype=jnp.int32)
    row_total = CUBES_DEV * HEADS
    slot_total = N_TM * CAP

    def one_device(device, device_subkey):
        subkeys = jax.random.split(device_subkey, 5)
        target = jnp.where(full_owner == device, (full_owner + 1) % N_TM, full_owner)
        slot_owner = jnp.arange(slot_total, dtype=jnp.int32) // CAP
        priority = jax.random.permutation(subkeys[0], slot_total).astype(jnp.int32)
        priority = jnp.where(slot_owner == target, -1, priority)
        priority = jnp.where(slot_owner == device, slot_total + 1, priority)
        picked = jnp.argsort(priority, stable=True)[:REMOTE]
        remote_owner = slot_owner[picked]
        row_pick = jax.random.permutation(subkeys[1], row_total)[:REMOTE]
        list_slot = jax.random.randint(subkeys[2], (REMOTE,), 0, K_TOP, jnp.int32)
        remote_cube = jax.random.randint(subkeys[3], (REMOTE,), 0, CUBES_DEV, jnp.int32)
        row_keys = jax.random.split(subkeys[4], row_total)
        shuffled = jax.vmap(lambda row_key: jax.random.permutation(row_key, CUBES_DEV))(row_keys).astype(jnp.int32)
        columns = jnp.arange(K_TOP, dtype=jnp.int32) % CUBES_DEV
        listed = device * CUBES_DEV + shuffled[:, columns]
        listed = listed.at[row_pick, list_slot].set(remote_owner * CUBES_DEV + remote_cube)
        return listed.reshape(CUBES_DEV, HEADS, K_TOP)
    lists_all = jax.vmap(one_device)(device_ids, jax.random.split(device_key, N_TM))
    return lists_all.reshape(NC, HEADS, K_TOP).astype(jnp.int32)


def setup_inputs(seed: int = 0, part: int = 0) -> dict:
    splits = jax.random.split(jax.random.key(seed), 7)
    own_keys = jax.random.split(jax.random.fold_in(splits[6], part), 7)
    queries = draw_queries(jax.random.fold_in(jax.random.fold_in(splits[6], part), 71), part)
    keys = draw_keys(jax.random.fold_in(jax.random.fold_in(splits[6], part), 71), part)
    values = draw_values(jax.random.fold_in(jax.random.fold_in(splits[6], part), 71), part)
    block_lists = draw_block_lists(jax.random.fold_in(jax.random.fold_in(splits[6], part), 71), part)
    gate_coarse = jnp.clip(jnp.exp(jax.random.uniform(splits[4], (HEADS,), jnp.float32, math.log(0.5), math.log(2.0))), 0.5, 2.0)
    gate_fine = jnp.clip(jnp.exp(jax.random.uniform(splits[5], (HEADS,), jnp.float32, math.log(0.5), math.log(2.0))), 0.5, 2.0)
    return dict(queries=queries, keys=keys, values=values, block_lists=block_lists, gate_coarse=gate_coarse, gate_fine=gate_fine)


def softmax_rows(scores):
    largest = jnp.max(scores, axis=-1, keepdims=True)
    raised = jnp.exp(scores - largest)
    return raised / jnp.sum(raised, axis=-1, keepdims=True)


def pooled_of(tensor):
    shaped = tensor.reshape(NC, CUBE, HEADS, HEAD_DIM)
    return jnp.mean(shaped.astype(jnp.float32), axis=1).astype(jnp.bfloat16)


def reference(queries, keys, values, block_lists, gate_coarse, gate_fine):
    score_scale = HEAD_DIM ** -0.5
    pooled_queries = pooled_of(queries)
    pooled_keys = pooled_of(keys)
    pooled_values = pooled_of(values)
    coarse_scores = jnp.einsum("chd,jhd->chj", pooled_queries.astype(jnp.float32), pooled_keys.astype(jnp.float32)) * score_scale
    coarse_weights = softmax_rows(coarse_scores).astype(jnp.bfloat16)
    coarse = jnp.einsum("chj,jhd->chd", coarse_weights.astype(jnp.float32), pooled_values.astype(jnp.float32))
    query_cubes = queries.reshape(NC, CUBE, HEADS, HEAD_DIM)
    key_heads = keys.reshape(NC, CUBE, HEADS, HEAD_DIM).transpose(0, 2, 1, 3)
    value_heads = values.reshape(NC, CUBE, HEADS, HEAD_DIM).transpose(0, 2, 1, 3)
    head_column = jnp.arange(HEADS, dtype=jnp.int32)[:, None]

    def attend(block_item):
        query_cube, listed = block_item
        listed = listed.astype(jnp.int32)
        key_block = key_heads[listed, head_column]
        value_block = value_heads[listed, head_column].reshape(HEADS, K_TOP * CUBE, HEAD_DIM)
        fine_scores = jnp.einsum("qhd,hksd->hqks", query_cube.astype(jnp.float32), key_block.astype(jnp.float32)) * score_scale
        fine_weights = softmax_rows(fine_scores.reshape(HEADS, CUBE, K_TOP * CUBE)).astype(jnp.bfloat16)
        return jnp.einsum("hqn,hnd->qhd", fine_weights.astype(jnp.float32), value_block.astype(jnp.float32))

    fine_out = lax.map(attend, (query_cubes, block_lists))
    blended = gate_coarse[None, None, :, None] * coarse[:, None, :, :] + gate_fine[None, None, :, None] * fine_out
    return blended.reshape(NTOK, HEADS * HEAD_DIM).astype(jnp.bfloat16)
```

```python
import functools
import math

import jax
import jax.numpy as jnp
from jax import lax
from jax.experimental import pallas as pl
from jax.experimental.pallas import tpu as pltpu
from jax.sharding import PartitionSpec as P

CUBE = 64
CAP = 4
LOG2E = math.log2(math.e)
LANES = 128
PATCH_BATCH = 6
PRE_BATCH = 2
MB = 1024 * 1024
F32 = jnp.float32
BF16 = jnp.bfloat16
I32 = jnp.int32


def vmem():
    return pl.BlockSpec(memory_space=pltpu.VMEM)


def smem():
    return pl.BlockSpec(memory_space=pltpu.SMEM)


def anywhere():
    return pl.BlockSpec(memory_space=pl.ANY)


def dot_t(a, b):
    return lax.dot_general(a, b, (((1,), (1,)), ((), ())), preferred_element_type=F32)


def dot_n(a, b):
    return lax.dot_general(a, b, (((1,), (0,)), ((), ())), preferred_element_type=F32)


def row_bits(head_count):
    return (head_count - 1).bit_length()


def plan_kernel(lists_ref, codes_ref, meta_ref):
    me = lax.axis_index("tm")
    lists = lists_ref[...]
    cube_count, list_len, head_count = lists.shape
    device_count = codes_ref.shape[0]
    cube_bits = cube_count.bit_length() - 1
    shift = row_bits(head_count)
    far = lax.shift_right_arithmetic(lists, cube_bits) != me
    local = lists & (cube_count - 1)
    far_value = jnp.max(jnp.where(far, lists, -1), axis=1)
    near_set = jnp.sum(jnp.where(far, 0, lax.shift_left(jnp.ones_like(local), local)), axis=1)
    grid = (device_count, cube_count, head_count)
    flat = (device_count * cube_count, head_count)
    owner = lax.broadcasted_iota(I32, grid, 0)
    cube = lax.broadcasted_iota(I32, grid, 1)
    head = lax.broadcasted_iota(I32, grid, 2)
    value = jnp.broadcast_to(far_value[None], grid)
    hit = jnp.where(lax.shift_right_arithmetic(value, cube_bits) == owner, 1.0, 0.0)
    hit = hit.astype(F32).reshape(flat)
    code = (lax.shift_left(value & (cube_count - 1), shift) | head).astype(F32).reshape(flat)
    row = ((lax.shift_left(cube, shift) | head) + 1).astype(F32).reshape(flat)
    kept = jnp.broadcast_to(near_set[None], grid).astype(F32).reshape(flat)
    square = (head_count, head_count)
    before = lax.broadcasted_iota(I32, square, 0) < lax.broadcasted_iota(I32, square, 1)
    hit_b = hit.astype(BF16)
    rank = dot_n(hit_b, jnp.where(before, 1.0, 0.0).astype(BF16))
    total = dot_n(hit_b, jnp.ones(square, BF16))
    block = (flat[0], flat[0])
    high = lax.broadcasted_iota(I32, block, 0)
    low = lax.broadcasted_iota(I32, block, 1)
    same = lax.shift_right_logical(high, cube_bits) == lax.shift_right_logical(low, cube_bits)
    rank = rank + dot_n(jnp.where(same & (low < high), 1.0, 0.0).astype(BF16), total.astype(BF16))
    lane = lax.broadcasted_iota(I32, (head_count, LANES), 1)
    codes = jnp.zeros((flat[0], LANES), F32)
    meta = jnp.zeros((flat[0], LANES), F32)
    for slot in range(CAP):
        chosen = jnp.where(rank == float(slot), hit, 0.0)
        at_slot = jnp.where(lane == slot, 1.0, 0.0).astype(BF16)
        at_set = jnp.where(lane == slot + CAP, 1.0, 0.0).astype(BF16)
        codes = codes + dot_n((chosen * code).astype(BF16), at_slot)
        meta = meta + dot_n((chosen * row).astype(BF16), at_slot)
        meta = meta + dot_n((chosen * kept).astype(BF16), at_set)
    shape = (device_count, cube_count, LANES)
    codes_ref[...] = jnp.sum(codes.reshape(shape), axis=1).astype(I32)
    meta_ref[...] = jnp.sum(meta.reshape(shape), axis=1).astype(I32)


def plan(block_lists, device_count):
    lists = jnp.transpose(block_lists, (0, 2, 1))
    out = jax.ShapeDtypeStruct((device_count, LANES), I32)
    return pl.pallas_call(
        plan_kernel,
        out_shape=(out, out),
        in_specs=[vmem()],
        out_specs=(vmem(), vmem()),
        name="plan",
        cost_estimate=pl.CostEstimate(flops=1000000, bytes_accessed=64 * 1024, transcendentals=0),
    )(lists)


def gather_kernel(shift, codes_ref, keys_ref, values_ref, tiles_ref, done_ref, sem):
    device_count, _, _, rows, width = tiles_ref.shape

    @pl.loop(0, device_count)
    def _(peer):
        for slot in range(CAP):
            code = codes_ref[peer, slot]
            cube = lax.shift_right_logical(code, shift)
            head = code & ((1 << shift) - 1)
            where = (
                pl.ds(pl.multiple_of(cube * rows, rows), rows),
                pl.ds(pl.multiple_of(head * width, width), width),
            )
            pltpu.make_async_copy(keys_ref.at[where], tiles_ref.at[peer, slot, 0], sem).start()
            pltpu.make_async_copy(values_ref.at[where], tiles_ref.at[peer, slot, 1], sem).start()

    done_ref[...] = jnp.zeros_like(done_ref)
    pltpu.make_async_copy(tiles_ref, tiles_ref, sem).wait()


def gather_tiles(codes, keys, values, head_count):
    device_count = codes.shape[0]
    width = keys.shape[1] // head_count
    shape = (device_count, CAP, 2, CUBE, width)
    return pl.pallas_call(
        functools.partial(gather_kernel, row_bits(head_count)),
        out_shape=(
            jax.ShapeDtypeStruct(shape, BF16),
            jax.ShapeDtypeStruct((8, LANES), F32),
        ),
        in_specs=[smem(), anywhere(), anywhere()],
        out_specs=(anywhere(), vmem()),
        scratch_shapes=[pltpu.SemaphoreType.DMA],
        name="gather_tiles",
        cost_estimate=pl.CostEstimate(
            flops=0, bytes_accessed=4 * math.prod(shape), transcendentals=0
        ),
    )(codes, keys, values)


def pool_kernel(q_ref, k_ref, v_ref, pq_ref, pkv_ref):
    for source, target in ((q_ref, pq_ref), (k_ref, pkv_ref.at[0]), (v_ref, pkv_ref.at[1])):
        tokens, columns = source.shape
        cubes = tokens // CUBE
        mean = jnp.sum(source[...].astype(F32).reshape(cubes, CUBE, columns), axis=1) * (1.0 / CUBE)
        target[...] = mean.astype(BF16)


def pool(queries, keys, values, cube_count):
    tokens, columns = queries.shape
    step = columns // 5
    block = pl.BlockSpec((tokens, step), lambda i: (0, i))
    return pl.pallas_call(
        pool_kernel,
        out_shape=(
            jax.ShapeDtypeStruct((cube_count, columns), BF16),
            jax.ShapeDtypeStruct((2, cube_count, columns), BF16),
        ),
        grid=(5,),
        in_specs=[block] * 3,
        out_specs=(
            pl.BlockSpec((cube_count, step), lambda i: (0, i)),
            pl.BlockSpec((2, cube_count, step), lambda i: (0, 0, i)),
        ),
        name="pool",
        compiler_params=pltpu.CompilerParams(vmem_limit_bytes=32 * MB),
        cost_estimate=pl.CostEstimate(
            flops=3 * tokens * columns, bytes_accessed=6 * tokens * columns, transcendentals=0
        ),
    )(queries, keys, values)


def near_kernel(scale, q_ref, k_ref, v_ref, after_ref, out_ref):
    tokens = q_ref.shape[0]
    keys = k_ref[...]
    values = v_ref[...]
    step = 128
    for start in range(0, tokens, step):
        scores = dot_t(q_ref[start : start + step, :], keys)
        largest = jnp.max(scores, axis=1, keepdims=True)
        raised = jnp.exp2((scores - largest) * scale)
        total = jnp.sum(raised, axis=1, keepdims=True)
        mixed = dot_n(raised.astype(BF16), values)
        out_ref[start : start + step, :] = mixed / total


def near_attention(queries, keys, values, after, head_count):
    tokens, columns = queries.shape
    width = columns // head_count
    block = pl.BlockSpec((tokens, width), lambda i: (0, i))
    return pl.pallas_call(
        functools.partial(near_kernel, width**-0.5 * LOG2E),
        out_shape=jax.ShapeDtypeStruct((tokens, columns), F32),
        grid=(head_count,),
        in_specs=[block] * 3 + [anywhere()],
        out_specs=block,
        name="near_attention",
        compiler_params=pltpu.CompilerParams(vmem_limit_bytes=32 * MB),
        cost_estimate=pl.CostEstimate(
            flops=4 * tokens * tokens * columns,
            bytes_accessed=10 * tokens * columns,
            transcendentals=tokens * tokens * head_count,
        ),
    )(queries, keys, values, after)


def pre_kernel(
    scale,
    shift,
    meta_ref,
    q_ref,
    k_ref,
    v_ref,
    after_ref,
    count_ref,
    slots_ref,
    rows_ref,
    queries_ref,
    mixed_ref,
    largest_ref,
    total_ref,
    sets_ref,
):
    device_count = meta_ref.shape[0]
    width = queries_ref.shape[2]
    tokens = q_ref.shape[0]
    last = slots_ref.shape[0]

    def clear(i, carry):
        slots_ref[i] = 0
        rows_ref[i] = 0
        sets_ref[i] = 1
        return carry

    lax.fori_loop(0, last, clear, 0)

    def scan(peer, found):
        for slot in range(CAP):
            row = meta_ref[peer, slot]

            @pl.when(row > 0)
            def _():
                slots_ref[found] = peer * CAP + slot
                rows_ref[found] = row - 1
                sets_ref[found] = meta_ref[peer, slot + CAP]

            found = found + (row > 0).astype(I32)
        return found

    found = lax.fori_loop(0, device_count, scan, jnp.int32(0))
    count_ref[0] = found
    cube_of = lax.broadcasted_iota(I32, (1, tokens), 1) // CUBE

    @pl.loop(0, pl.cdiv(found, PRE_BATCH))
    def _(step):
        for part in range(PRE_BATCH):
            i = step * PRE_BATCH + part
            row = rows_ref[i]
            cube = lax.shift_right_logical(row, shift)
            head = row & ((1 << shift) - 1)
            columns = pl.ds(pl.multiple_of(head * width, width), width)
            queries = q_ref[pl.ds(pl.multiple_of(cube * CUBE, CUBE), CUBE), columns]
            kept = (lax.shift_right_logical(sets_ref[i], cube_of) & 1) > 0
            scores = dot_t(queries, k_ref[:, columns])
            scores = jnp.where(kept, scores, -3e38)
            largest = jnp.max(scores, axis=1, keepdims=True)
            raised = jnp.exp2((scores - largest) * scale)
            total = jnp.sum(raised, axis=1, keepdims=True)
            queries_ref[i] = queries
            mixed_ref[i] = dot_n(raised.astype(BF16), v_ref[:, columns])
            largest_ref[i] = jnp.broadcast_to(largest, (CUBE, width))
            total_ref[i] = jnp.broadcast_to(total, (CUBE, width))


def far_rows(meta, queries, keys, values, after, head_count):
    device_count = meta.shape[0]
    tokens, columns = queries.shape
    width = columns // head_count
    slot_count = device_count * CAP
    dense = slot_count + PATCH_BATCH
    tile = (dense, CUBE, width)
    return pl.pallas_call(
        functools.partial(pre_kernel, width**-0.5 * LOG2E, row_bits(head_count)),
        out_shape=(
            jax.ShapeDtypeStruct((1,), I32),
            jax.ShapeDtypeStruct((dense,), I32),
            jax.ShapeDtypeStruct((dense,), I32),
            jax.ShapeDtypeStruct(tile, BF16),
            jax.ShapeDtypeStruct(tile, F32),
            jax.ShapeDtypeStruct(tile, F32),
            jax.ShapeDtypeStruct(tile, F32),
        ),
        in_specs=[smem(), vmem(), vmem(), vmem(), anywhere()],
        out_specs=(smem(), smem(), smem(), vmem(), vmem(), vmem(), vmem()),
        scratch_shapes=[pltpu.SMEM((dense,), I32)],
        name="far_rows",
        compiler_params=pltpu.CompilerParams(vmem_limit_bytes=40 * MB),
        cost_estimate=pl.CostEstimate(
            flops=4 * slot_count * CUBE * tokens * width,
            bytes_accessed=6 * tokens * columns,
            transcendentals=slot_count * CUBE * tokens,
        ),
    )(meta, queries, keys, values, after)


def blend_kernel(scale, heads, gc_ref, gf_ref, pq_ref, pk_ref, pv_ref, near_ref, out_ref, coarse_ref):
    device_count, _, cube_count, columns = pk_ref.shape
    width = columns // heads
    first = pl.program_id(0) * heads
    every = device_count * cube_count
    for part in range(heads):
        here = slice(part * width, (part + 1) * width)
        keys = pk_ref[:, 0, :, here].reshape(every, width)
        values = pv_ref[:, 0, :, here].reshape(every, width)
        scores = dot_t(pq_ref[:, here], keys) * scale
        largest = jnp.max(scores, axis=1, keepdims=True)
        raised = jnp.exp(scores - largest)
        weights = (raised / jnp.sum(raised, axis=1, keepdims=True)).astype(BF16)
        coarse = gc_ref[first + part] * dot_n(weights, values)
        coarse_ref[:, here] = coarse
        near = near_ref[:, here].reshape(cube_count, CUBE, width)
        blended = coarse[:, None, :] + gf_ref[first + part] * near
        out_ref[:, here] = blended.reshape(cube_count * CUBE, width).astype(BF16)


def blend(gate_coarse, gate_fine, pooled_queries, every, near, head_count):
    tokens, columns = near.shape
    cube_count = pooled_queries.shape[0]
    device_count = every.shape[0]
    width = columns // head_count
    heads = 4 if head_count % 4 == 0 else 1
    step = heads * width
    return pl.pallas_call(
        functools.partial(blend_kernel, width**-0.5, heads),
        out_shape=(
            jax.ShapeDtypeStruct((tokens, columns), BF16),
            jax.ShapeDtypeStruct((cube_count, columns), F32),
        ),
        grid=(head_count // heads,),
        in_specs=[
            smem(),
            smem(),
            pl.BlockSpec((cube_count, step), lambda i: (0, i)),
            pl.BlockSpec((device_count, 1, cube_count, step), lambda i: (0, 0, 0, i)),
            pl.BlockSpec((device_count, 1, cube_count, step), lambda i: (0, 1, 0, i)),
            pl.BlockSpec((tokens, step), lambda i: (0, i)),
        ],
        out_specs=(
            pl.BlockSpec((tokens, step), lambda i: (0, i)),
            pl.BlockSpec((cube_count, step), lambda i: (0, i)),
        ),
        name="blend",
        compiler_params=pltpu.CompilerParams(vmem_limit_bytes=32 * MB),
        cost_estimate=pl.CostEstimate(
            flops=2 * tokens * columns, bytes_accessed=6 * tokens * columns, transcendentals=0
        ),
    )(gate_coarse, gate_fine, pooled_queries, every, every, near)


def patch_kernel(
    scale,
    shift,
    count_ref,
    slots_ref,
    rows_ref,
    gf_ref,
    tiles_ref,
    queries_ref,
    mixed_ref,
    largest_ref,
    total_ref,
    coarse_ref,
    base_ref,
    out_ref,
    ready_ref,
    sems,
):
    width = queries_ref.shape[2]
    count = count_ref[0]

    def copy_of(i):
        row = rows_ref[i]
        cube = lax.shift_right_logical(row, shift)
        head = row & ((1 << shift) - 1)
        target = out_ref.at[
            pl.ds(pl.multiple_of(cube * CUBE, CUBE), CUBE),
            pl.ds(pl.multiple_of(head * width, width), width),
        ]
        return pltpu.make_async_copy(ready_ref.at[i], target, sems.at[i])

    @pl.loop(0, pl.cdiv(count, PATCH_BATCH))
    def _(step):
        for part in range(PATCH_BATCH):
            i = step * PATCH_BATCH + part
            slot = slots_ref[i]
            row = rows_ref[i]
            cube = lax.shift_right_logical(row, shift)
            head = row & ((1 << shift) - 1)
            scores = dot_t(queries_ref[i], tiles_ref[slot, 0])
            near_top = largest_ref[i][:, :1]
            largest = jnp.maximum(near_top, jnp.max(scores, axis=1, keepdims=True))
            raised = jnp.exp2((scores - largest) * scale)
            kept = jnp.exp2((near_top - largest) * scale)
            total = total_ref[i][:, :1] * kept + jnp.sum(raised, axis=1, keepdims=True)
            mixed = mixed_ref[i] * kept + dot_n(raised.astype(BF16), tiles_ref[slot, 1])
            columns = pl.ds(pl.multiple_of(head * width, width), width)
            coarse = coarse_ref[:, columns]
            this_cube = lax.broadcasted_iota(I32, coarse.shape, 0) == cube
            coarse = jnp.sum(jnp.where(this_cube, coarse, 0.0), axis=0, keepdims=True)
            ready_ref[i] = (coarse + mixed * (gf_ref[head] / total)).astype(BF16)
        for part in range(PATCH_BATCH):
            i = step * PATCH_BATCH + part

            @pl.when(i < count)
            def _():
                copy_of(i).start()

    @pl.loop(0, count)
    def _(i):
        copy_of(i).wait()


def patch(listed, gate_fine, tiles, parts, coarse, base, head_count):
    count, slots, rows = listed
    dense = slots.shape[0]
    tokens, columns = base.shape
    width = columns // head_count
    return pl.pallas_call(
        functools.partial(patch_kernel, width**-0.5 * LOG2E, row_bits(head_count)),
        out_shape=jax.ShapeDtypeStruct((tokens, columns), BF16),
        in_specs=[smem()] * 4 + [vmem()] * 6 + [anywhere()],
        out_specs=anywhere(),
        scratch_shapes=[
            pltpu.VMEM((dense, CUBE, width), BF16),
            pltpu.SemaphoreType.DMA((dense,)),
        ],
        input_output_aliases={10: 0},
        name="patch",
        compiler_params=pltpu.CompilerParams(vmem_limit_bytes=40 * MB),
        cost_estimate=pl.CostEstimate(
            flops=4 * dense * CUBE * CUBE * width,
            bytes_accessed=16 * dense * CUBE * width,
            transcendentals=dense * CUBE * CUBE,
        ),
    )(count, slots, rows, gate_fine, tiles, *parts, coarse, base)


def per_device(queries, keys, values, block_lists, gate_coarse, gate_fine):
    head_count = gate_coarse.shape[0]
    width = queries.shape[1] // head_count
    cube_count = block_lists.shape[0]
    device_count = lax.axis_size("tm")
    codes, meta = plan(block_lists, device_count)
    wanted = lax.all_to_all(codes, "tm", split_axis=0, concat_axis=0, tiled=True)
    pooled_queries, pooled_pairs = pool(queries, keys, values, cube_count)
    every = lax.all_gather(pooled_pairs, "tm", axis=0, tiled=False)
    tiles, after = gather_tiles(wanted, keys, values, head_count)
    fetched = lax.all_to_all(tiles, "tm", split_axis=0, concat_axis=0, tiled=True)
    near = near_attention(queries, keys, values, after, head_count)
    pre = far_rows(meta, queries, keys, values, after, head_count)
    base, coarse = blend(gate_coarse, gate_fine, pooled_queries, every, near, head_count)
    fetched = fetched.reshape(device_count * CAP, 2, CUBE, width)
    return patch(pre[:3], gate_fine, fetched, pre[3:], coarse, base, head_count)


def solution(mesh):
    return jax.shard_map(
        per_device,
        mesh=mesh,
        in_specs=(
            P(("groups", "tm"), None),
            P(("groups", "tm"), None),
            P(("groups", "tm"), None),
            P(("groups", "tm"), None, None),
            P(),
            P(),
        ),
        out_specs=P(("groups", "tm"), None),
        check_vma=False,
    )
```

```python
import functools
import math

import jax
import jax.numpy as jnp
from jax import lax
from jax.experimental import pallas as pl
from jax.experimental.pallas import tpu as pltpu
from jax.sharding import PartitionSpec as P

CUBE = 64
CAP = 4
LOG2E = math.log2(math.e)
LANES = 128
PATCH_BATCH = 10
PRE_BATCH = 5
NEAR_STEP = 256
NEAR_WEIGHT = 20
GATHER_WEIGHT = 20
MB = 1024 * 1024
SMALL = 6 * MB
LARGE = 56 * MB
F32 = jnp.float32
BF16 = jnp.bfloat16
I32 = jnp.int32


def vmem():
    return pl.BlockSpec(memory_space=pltpu.VMEM)


def smem():
    return pl.BlockSpec(memory_space=pltpu.SMEM)


def anywhere():
    return pl.BlockSpec(memory_space=pl.ANY)


def dot_t(a, b):
    return lax.dot_general(a, b, (((1,), (1,)), ((), ())), preferred_element_type=F32)


def dot_n(a, b):
    return lax.dot_general(a, b, (((1,), (0,)), ((), ())), preferred_element_type=F32)


def row_bits(head_count):
    return (head_count - 1).bit_length()


def plan_kernel(lists_hbm, codes_ref, slots_ref, kept_ref, lists_ref, sem):
    lists_load = pltpu.make_async_copy(lists_hbm, lists_ref, sem)
    lists_load.start()
    lists_load.wait()
    me = lax.axis_index("tm")
    lists = lists_ref[...]
    cube_count, list_len, head_count = lists.shape
    device_count = codes_ref.shape[0]
    cube_bits = cube_count.bit_length() - 1
    shift = row_bits(head_count)
    far = lax.shift_right_arithmetic(lists, cube_bits) != me
    local = lists & (cube_count - 1)
    far_value = jnp.max(jnp.where(far, lists, -1), axis=1)
    bits = jnp.where(far, 0, lax.shift_left(jnp.ones_like(local), local))
    kept_ref[...] = jnp.sum(bits, axis=1)
    grid = (device_count, cube_count, head_count)
    flat = (device_count * cube_count, head_count)
    owner = lax.broadcasted_iota(I32, grid, 0)
    head = lax.broadcasted_iota(I32, grid, 2)
    value = jnp.broadcast_to(far_value[None], grid)
    hit = jnp.where(lax.shift_right_arithmetic(value, cube_bits) == owner, 1.0, 0.0)
    hit = hit.astype(F32).reshape(flat)
    code = (lax.shift_left(value & (cube_count - 1), shift) | head).astype(F32).reshape(flat)
    square = (head_count, head_count)
    before = lax.broadcasted_iota(I32, square, 0) < lax.broadcasted_iota(I32, square, 1)
    hit_b = hit.astype(BF16)
    rank = dot_n(hit_b, jnp.where(before, 1.0, 0.0).astype(BF16))
    total = dot_n(hit_b, jnp.ones(square, BF16))
    block = (flat[0], flat[0])
    high = lax.broadcasted_iota(I32, block, 0)
    low = lax.broadcasted_iota(I32, block, 1)
    same = lax.shift_right_logical(high, cube_bits) == lax.shift_right_logical(low, cube_bits)
    rank = rank + dot_n(jnp.where(same & (low < high), 1.0, 0.0).astype(BF16), total.astype(BF16))
    lane = lax.broadcasted_iota(I32, (head_count, LANES), 1)
    codes = jnp.zeros((flat[0], LANES), F32)
    for slot in range(CAP):
        chosen = jnp.where(rank == float(slot), hit, 0.0)
        at_slot = jnp.where(lane == slot, 1.0, 0.0).astype(BF16)
        codes = codes + dot_n((chosen * (code + 1.0)).astype(BF16), at_slot)
    codes = jnp.sum(codes.reshape(device_count, cube_count, LANES), axis=1)
    codes_ref[...] = codes.astype(I32)
    slot_of = owner.astype(F32) * CAP + rank.reshape(grid) + 1.0
    slots_ref[...] = jnp.sum(slot_of * hit.reshape(grid), axis=0).astype(I32)


def plan(block_lists, device_count):
    lists = jnp.transpose(block_lists, (0, 2, 1))
    rows = jax.ShapeDtypeStruct(block_lists.shape[:2], I32)
    return pl.pallas_call(
        plan_kernel,
        out_shape=(jax.ShapeDtypeStruct((device_count, LANES), I32), rows, rows),
        in_specs=[anywhere()],
        out_specs=(vmem(),) * 3,
        scratch_shapes=[pltpu.VMEM(lists.shape, I32), pltpu.SemaphoreType.DMA],
        name="plan",
        compiler_params=pltpu.CompilerParams(vmem_limit_bytes=LARGE),
        cost_estimate=pl.CostEstimate(flops=1000000, bytes_accessed=64 * 1024, transcendentals=0),
    )(lists)


def pool_kernel(k_hbm, v_hbm, after_ref, pooled_ref, k_ref, v_ref, sums_ref, sems):
    cubes = pooled_ref.shape[1]
    loads = {}
    for cube in range(cubes):
        where = pl.ds(cube * CUBE, CUBE)
        for i, (source, target) in enumerate(((k_hbm, k_ref), (v_hbm, v_ref))):
            load = pltpu.make_async_copy(source.at[where], target.at[where], sems.at[i, cube])
            load.start()
            loads[i, cube] = load
    for cube in range(cubes):
        for i, target in enumerate((k_ref, v_ref)):
            loads[i, cube].wait()
            tokens = target[cube * CUBE : (cube + 1) * CUBE, :].astype(F32)
            sums_ref[i, cube : cube + 1, :] = jnp.sum(tokens, axis=0, keepdims=True)
    for i in range(2):
        pooled_ref[i] = (sums_ref[i] * (1.0 / CUBE)).astype(BF16)


def pool(keys, values, after):
    tokens, columns = keys.shape
    cubes = tokens // CUBE
    return pl.pallas_call(
        pool_kernel,
        out_shape=jax.ShapeDtypeStruct((2, cubes, columns), BF16),
        in_specs=[anywhere()] * 3,
        out_specs=vmem(),
        scratch_shapes=[
            pltpu.VMEM((tokens, columns), BF16),
            pltpu.VMEM((tokens, columns), BF16),
            pltpu.VMEM((2, cubes, columns), F32),
            pltpu.SemaphoreType.DMA((2, cubes)),
        ],
        name="pool",
        compiler_params=pltpu.CompilerParams(vmem_limit_bytes=LARGE),
        cost_estimate=pl.CostEstimate(
            flops=2 * keys.size, bytes_accessed=4 * keys.size, transcendentals=0
        ),
    )(keys, values, after)


def gather_kernel(
    shift, codes_ref, k_hbm, v_hbm, after_ref, tiles_ref, done_ref, work_ref, load_sems, store_sems
):
    device_count, _, _, rows, width = tiles_ref.shape

    def each(act):
        @pl.loop(0, device_count)
        def _(peer):
            for slot in range(CAP):
                code = codes_ref[peer, slot] - 1
                pl.when(code >= 0)(functools.partial(act, peer, slot, code))

    def load(peer, slot, code):
        cube = lax.shift_right_logical(code, shift)
        head = code & ((1 << shift) - 1)
        where = (
            pl.ds(pl.multiple_of(cube * rows, rows), rows),
            pl.ds(pl.multiple_of(head * width, width), width),
        )
        for i, source in enumerate((k_hbm, v_hbm)):
            pltpu.make_async_copy(
                source.at[where], work_ref.at[peer, slot, i], load_sems.at[peer, slot]
            ).start()

    def store_of(peer, slot):
        return pltpu.make_async_copy(
            work_ref.at[peer, slot], tiles_ref.at[peer, slot], store_sems.at[peer, slot]
        )

    def store(peer, slot, code):
        both = work_ref.at[peer, slot]
        pltpu.make_async_copy(both, both, load_sems.at[peer, slot]).wait()
        store_of(peer, slot).start()

    def finish(peer, slot, code):
        store_of(peer, slot).wait()

    each(load)
    done_ref[...] = jnp.zeros_like(done_ref)
    each(store)
    each(finish)


def gather_tiles(codes, keys, values, after, head_count):
    device_count = codes.shape[0]
    tokens, columns = keys.shape
    shape = (device_count, CAP, 2, CUBE, columns // head_count)
    return pl.pallas_call(
        functools.partial(gather_kernel, row_bits(head_count)),
        out_shape=(
            jax.ShapeDtypeStruct(shape, BF16),
            jax.ShapeDtypeStruct((8, LANES), F32),
        ),
        in_specs=[smem()] + [anywhere()] * 3,
        out_specs=(anywhere(), vmem()),
        scratch_shapes=[
            pltpu.VMEM(shape, BF16),
            pltpu.SemaphoreType.DMA((device_count, CAP)),
            pltpu.SemaphoreType.DMA((device_count, CAP)),
        ],
        name="gather_tiles",
        compiler_params=pltpu.CompilerParams(vmem_limit_bytes=LARGE),
        cost_estimate=pl.CostEstimate(
            flops=0, bytes_accessed=GATHER_WEIGHT * 4 * math.prod(shape), transcendentals=0
        ),
    )(codes, keys, values, after)


def join_kernel(piece_count, *refs):
    out_ref = refs[-1]
    start = 0
    for piece in refs[:piece_count]:
        out_ref[start : start + piece.shape[0]] = piece[...]
        start += piece.shape[0]


def join(pieces, after=()):
    shape = (sum(piece.shape[0] for piece in pieces),) + pieces[0].shape[1:]
    return pl.pallas_call(
        functools.partial(join_kernel, len(pieces)),
        out_shape=jax.ShapeDtypeStruct(shape, BF16),
        in_specs=[vmem()] * len(pieces) + [anywhere()] * len(after),
        out_specs=vmem(),
        name="join",
        compiler_params=pltpu.CompilerParams(vmem_limit_bytes=SMALL),
        cost_estimate=pl.CostEstimate(
            flops=0, bytes_accessed=4 * math.prod(shape), transcendentals=0
        ),
    )(*pieces, *after)


def near_kernel(scale, q_ref, k_ref, v_ref, after_ref, out_ref, pooled_ref):
    tokens, width = q_ref.shape
    cubes = pooled_ref.shape[0]
    sums = jnp.sum(q_ref[...].astype(F32).reshape(cubes, CUBE, width), axis=1)
    pooled_ref[...] = (sums * (1.0 / CUBE)).astype(BF16)
    keys = k_ref[...]
    values = jnp.concatenate([v_ref[...], jnp.ones(v_ref.shape, BF16)], axis=1)
    step = NEAR_STEP
    starts = range(0, tokens, step)
    scores = dot_t(q_ref[0:step, :], keys)
    for start in starts:
        following = start + step
        if following < tokens:
            next_scores = dot_t(q_ref[following : following + step, :], keys)
        largest = jnp.max(scores, axis=1, keepdims=True)
        raised = jnp.exp2((scores - largest) * scale)
        mixed = dot_n(raised.astype(BF16), values)
        out_ref[start : start + step, :] = mixed[:, :width] / mixed[:, width:]
        if following < tokens:
            scores = next_scores


def near_attention(queries, keys, values, after, first, heads, width):
    tokens = queries.shape[0]
    block = pl.BlockSpec((tokens, width), lambda i: (0, first + i))
    return pl.pallas_call(
        functools.partial(near_kernel, width**-0.5 * LOG2E),
        out_shape=(
            jax.ShapeDtypeStruct((tokens, heads * width), F32),
            jax.ShapeDtypeStruct((tokens // CUBE, heads * width), BF16),
        ),
        grid=(heads,),
        in_specs=[block] * 3 + [anywhere()],
        out_specs=(
            pl.BlockSpec((tokens, width), lambda i: (0, i)),
            pl.BlockSpec((tokens // CUBE, width), lambda i: (0, i)),
        ),
        name="near_attention",
        compiler_params=pltpu.CompilerParams(vmem_limit_bytes=SMALL),
        cost_estimate=pl.CostEstimate(
            flops=NEAR_WEIGHT * 4 * tokens * tokens * heads * width,
            bytes_accessed=10 * tokens * heads * width,
            transcendentals=tokens * tokens * heads,
        ),
    )(queries, keys, values, after)


def pre_kernel(
    scale,
    shift,
    slot_of_ref,
    kept_ref,
    q_ref,
    k_ref,
    v_ref,
    after_ref,
    count_ref,
    slots_ref,
    rows_ref,
    queries_ref,
    mixed_ref,
    sums_ref,
    sets_ref,
):
    cube_count, head_count = slot_of_ref.shape
    width = queries_ref.shape[2]
    tokens = q_ref.shape[0]
    slots_ref[0] = 1
    rows_ref[0] = 0
    sets_ref[0] = 1

    def scan(cube, found):
        for head in range(head_count):
            slot = slot_of_ref[cube, head]
            slots_ref[found] = slot
            rows_ref[found] = lax.shift_left(cube, shift) | head
            sets_ref[found] = kept_ref[cube, head]
            found = found + (slot > 0).astype(I32)
        return found

    found = lax.fori_loop(0, cube_count, scan, jnp.int32(0))
    count_ref[0] = found
    last = jnp.maximum(found - 1, 0)
    for more in range(PATCH_BATCH):
        slots_ref[found + more] = slots_ref[last]
        rows_ref[found + more] = rows_ref[last]
        sets_ref[found + more] = sets_ref[last]
    cube_of = lax.broadcasted_iota(I32, (1, tokens), 1) // CUBE

    @pl.loop(0, pl.cdiv(found, PATCH_BATCH) * (PATCH_BATCH // PRE_BATCH))
    def _(step):
        first = step * PRE_BATCH
        parts = range(PRE_BATCH)
        codes = [rows_ref[first + part] for part in parts]
        cubes = [lax.shift_right_logical(code, shift) for code in codes]
        heads = [code & ((1 << shift) - 1) for code in codes]
        columns = [pl.ds(pl.multiple_of(head * width, width), width) for head in heads]
        queries = [
            q_ref[pl.ds(pl.multiple_of(cubes[part] * CUBE, CUBE), CUBE), columns[part]]
            for part in parts
        ]
        scores = [dot_t(queries[part], k_ref[:, columns[part]]) for part in parts]
        for part in parts:
            kept = (lax.shift_right_logical(sets_ref[first + part], cube_of) & 1) > 0
            scores[part] = jnp.where(kept, scores[part], -3e38)
        largest = [jnp.max(score, axis=1, keepdims=True) for score in scores]
        raised = [
            jnp.exp2((scores[part] - largest[part]) * scale).astype(BF16) for part in parts
        ]
        ones = jnp.ones((tokens, width), BF16)
        values = [jnp.concatenate([v_ref[:, columns[part]], ones], axis=1) for part in parts]
        mixed = [dot_n(raised[part], values[part]) for part in parts]
        for part in parts:
            queries_ref[first + part] = queries[part]
            total = mixed[part][:, width:]
            mixed_ref[first + part] = (mixed[part][:, :width] / total).astype(BF16)
            sums_ref[first + part] = largest[part] * scale + jnp.log2(total)


def far_rows(slot_of, kept, queries, keys, values, after, slot_count):
    tokens, columns = queries.shape
    head_count = slot_of.shape[1]
    width = columns // head_count
    dense = (slot_count // PATCH_BATCH + 2) * PATCH_BATCH
    tile = (dense, CUBE, width)
    return pl.pallas_call(
        functools.partial(pre_kernel, width**-0.5 * LOG2E, row_bits(head_count)),
        out_shape=(
            jax.ShapeDtypeStruct((1,), I32),
            jax.ShapeDtypeStruct((dense,), I32),
            jax.ShapeDtypeStruct((dense,), I32),
            jax.ShapeDtypeStruct(tile, BF16),
            jax.ShapeDtypeStruct(tile, BF16),
            jax.ShapeDtypeStruct(tile, F32),
        ),
        in_specs=[smem(), smem(), vmem(), vmem(), vmem(), anywhere()],
        out_specs=(smem(), smem(), smem(), vmem(), vmem(), vmem()),
        scratch_shapes=[pltpu.SMEM((dense,), I32)],
        name="far_rows",
        compiler_params=pltpu.CompilerParams(vmem_limit_bytes=SMALL),
        cost_estimate=pl.CostEstimate(
            flops=4 * slot_count * CUBE * tokens * width,
            bytes_accessed=6 * tokens * columns,
            transcendentals=slot_count * CUBE * tokens,
        ),
    )(slot_of, kept, queries, keys, values, after)


def blend_kernel(scale, heads, pieces, parts, gc_ref, gf_ref, *refs):
    key_refs, value_refs = refs[:pieces], refs[pieces : 2 * pieces]
    near_refs = refs[2 * pieces : 2 * pieces + parts]
    query_refs = refs[2 * pieces + parts : 2 * pieces + 2 * parts]
    out_ref, coarse_ref = refs[2 * pieces + 2 * parts :]
    cube_count, columns = coarse_ref.shape
    width = columns // heads
    first = pl.program_id(0) * heads
    places = [slice(part * width, (part + 1) * width) for part in range(heads)]

    def gathered(piece_refs, here):
        flat = [ref[:, 0, :, here].reshape(-1, width) for ref in piece_refs]
        return jnp.concatenate(flat, axis=0)

    def put(near_ref, query_ref):
        keys = [gathered(key_refs, here) for here in places]
        values = [gathered(value_refs, here) for here in places]
        scores = [dot_t(query_ref[:, here], key) for here, key in zip(places, keys)]
        scores = jnp.concatenate(scores, axis=0) * scale
        largest = jnp.max(scores, axis=1, keepdims=True)
        raised = jnp.exp(scores - largest)
        weights = raised / jnp.sum(raised, axis=1, keepdims=True)
        coarse = []
        for part in range(heads):
            mine = weights[part * cube_count : (part + 1) * cube_count].astype(BF16)
            coarse.append(gc_ref[first + part] * dot_n(mine, values[part]))
        for part, here in enumerate(places):
            coarse_ref[:, here] = coarse[part]
            near = near_ref[:, here].reshape(cube_count, CUBE, width)
            blended = coarse[part][:, None, :] + gf_ref[first + part] * near
            out_ref[:, here] = blended.reshape(cube_count * CUBE, width).astype(BF16)

    share = pl.num_programs(0) // parts
    for part in range(parts):
        chosen = functools.partial(put, near_refs[part], query_refs[part])
        pl.when(pl.program_id(0) // share == part)(chosen)


def blend(gate_coarse, gate_fine, pieces, nears, pooled_queries, heads, width):
    tokens, part_columns = nears[0].shape
    cube_count = tokens // CUBE
    columns = part_columns * len(nears)
    step = heads * width
    share = part_columns // step

    def piece_spec(piece, which):
        shape = (piece.shape[0], 1, cube_count, step)
        return pl.BlockSpec(shape, lambda i: (0, which, 0, i))

    def part_spec(rows, part):
        return pl.BlockSpec(
            (rows, step), lambda i: (0, jnp.clip(i - part * share, 0, share - 1))
        )

    parts = range(len(nears))
    return pl.pallas_call(
        functools.partial(blend_kernel, width**-0.5, heads, len(pieces), len(nears)),
        out_shape=(
            jax.ShapeDtypeStruct((tokens, columns), BF16),
            jax.ShapeDtypeStruct((cube_count, columns), F32),
        ),
        grid=(columns // step,),
        in_specs=[smem(), smem()]
        + [piece_spec(piece, 0) for piece in pieces]
        + [piece_spec(piece, 1) for piece in pieces]
        + [part_spec(tokens, part) for part in parts]
        + [part_spec(cube_count, part) for part in parts],
        out_specs=(
            pl.BlockSpec((tokens, step), lambda i: (0, i)),
            pl.BlockSpec((cube_count, step), lambda i: (0, i)),
        ),
        name="blend",
        compiler_params=pltpu.CompilerParams(vmem_limit_bytes=16 * MB),
        cost_estimate=pl.CostEstimate(
            flops=2 * tokens * columns, bytes_accessed=6 * tokens * columns, transcendentals=0
        ),
    )(gate_coarse, gate_fine, *pieces, *pieces, *nears, *pooled_queries)


def patch_kernel(
    scale,
    shift,
    count_ref,
    slots_ref,
    rows_ref,
    gf_ref,
    tiles_hbm,
    queries_hbm,
    mixed_hbm,
    sums_hbm,
    coarse_hbm,
    base_ref,
    out_ref,
    tiles_ref,
    queries_ref,
    mixed_ref,
    sums_ref,
    coarse_ref,
    ready_ref,
    tile_sems,
    batch_sems,
    coarse_sem,
    store_sems,
):
    width = queries_ref.shape[2]
    count = count_ref[0]
    steps = pl.cdiv(count, PATCH_BATCH)
    coarse_load = pltpu.make_async_copy(coarse_hbm, coarse_ref, coarse_sem)

    def tile_load(i):
        tile = tiles_hbm.at[slots_ref[i] - 1]
        return pltpu.make_async_copy(tile, tiles_ref.at[i], tile_sems.at[i])

    def batch_load(step, which):
        source, target = (
            (queries_hbm, queries_ref),
            (mixed_hbm, mixed_ref),
            (sums_hbm, sums_ref),
        )[which]
        where = pl.ds(step * PATCH_BATCH, PATCH_BATCH)
        return pltpu.make_async_copy(source.at[where], target.at[where], batch_sems.at[which, step])

    def store(i):
        row = rows_ref[i]
        cube = lax.shift_right_logical(row, shift)
        head = row & ((1 << shift) - 1)
        where = (
            pl.ds(pl.multiple_of(cube * CUBE, CUBE), CUBE),
            pl.ds(pl.multiple_of(head * width, width), width),
        )
        return pltpu.make_async_copy(ready_ref.at[i], out_ref.at[where], store_sems.at[i])

    @pl.loop(0, steps)
    def _(step):
        for part in range(PATCH_BATCH):
            tile_load(step * PATCH_BATCH + part).start()
        for which in range(3):
            batch_load(step, which).start()

        @pl.when(step == 0)
        def _():
            coarse_load.start()

    @pl.loop(0, steps)
    def _(step):
        @pl.when(step == 0)
        def _():
            coarse_load.wait()

        for which in range(3):
            batch_load(step, which).wait()
        first = step * PATCH_BATCH
        parts = range(PATCH_BATCH)
        for part in parts:
            tile_load(first + part).wait()
        codes = [rows_ref[first + part] for part in parts]
        cubes = [lax.shift_right_logical(code, shift) for code in codes]
        heads = [code & ((1 << shift) - 1) for code in codes]
        columns = [pl.ds(pl.multiple_of(head * width, width), width) for head in heads]
        scores = [dot_t(queries_ref[first + part], tiles_ref[first + part, 0]) for part in parts]
        scores = [score * scale for score in scores]
        tops = [jnp.max(score, axis=1, keepdims=True) for score in scores]
        sums = [sums_ref[first + part] for part in parts]
        largest = [jnp.maximum(sums[part], tops[part]) for part in parts]
        raised = [
            jnp.exp2(scores[part] - largest[part][:, :CUBE]).astype(BF16) for part in parts
        ]
        ones = jnp.ones((CUBE, width), BF16)
        values = [jnp.concatenate([tiles_ref[first + part, 1], ones], axis=1) for part in parts]
        mixed = [dot_n(raised[part], values[part]) for part in parts]
        for part in parts:
            coarse = coarse_ref[:, columns[part]]
            this_cube = lax.broadcasted_iota(I32, coarse.shape, 0) == cubes[part]
            coarse = jnp.sum(jnp.where(this_cube, coarse, 0.0), axis=0, keepdims=True)
            kept = jnp.exp2(sums[part] - largest[part])
            total = kept + mixed[part][:, width:]
            fine = mixed_ref[first + part].astype(F32) * kept + mixed[part][:, :width]
            blended = coarse + gf_ref[heads[part]] * (fine / total)
            ready_ref[first + part] = blended.astype(BF16)
        for part in parts:
            pl.when(first + part < count)(store(first + part).start)

    @pl.loop(0, count)
    def _(i):
        store(i).wait()


def patch(listed, gate_fine, tiles, parts, coarse, base):
    count, slots, rows = listed
    dense, _, width = parts[0].shape
    return pl.pallas_call(
        functools.partial(patch_kernel, width**-0.5 * LOG2E, row_bits(gate_fine.shape[0])),
        out_shape=jax.ShapeDtypeStruct(base.shape, BF16),
        in_specs=[smem()] * 4 + [anywhere()] * 6,
        out_specs=anywhere(),
        scratch_shapes=[
            pltpu.VMEM((dense,) + tiles.shape[1:], BF16),
            pltpu.VMEM((dense, CUBE, width), BF16),
            pltpu.VMEM((dense, CUBE, width), BF16),
            pltpu.VMEM((dense, CUBE, width), F32),
            pltpu.VMEM(coarse.shape, F32),
            pltpu.VMEM((dense, CUBE, width), BF16),
            pltpu.SemaphoreType.DMA((dense,)),
            pltpu.SemaphoreType.DMA((3, pl.cdiv(dense, PATCH_BATCH))),
            pltpu.SemaphoreType.DMA,
            pltpu.SemaphoreType.DMA((dense,)),
        ],
        input_output_aliases={9: 0},
        name="patch",
        compiler_params=pltpu.CompilerParams(vmem_limit_bytes=LARGE),
        cost_estimate=pl.CostEstimate(
            flops=4 * dense * CUBE * CUBE * width,
            bytes_accessed=16 * dense * CUBE * width,
            transcendentals=dense * CUBE * CUBE,
        ),
    )(count, slots, rows, gate_fine, tiles, *parts, coarse, base)


def per_device(queries, keys, values, block_lists, gate_coarse, gate_fine):
    head_count = gate_coarse.shape[0]
    width = queries.shape[1] // head_count
    cube_count = block_lists.shape[0]
    device_count = lax.axis_size("tm")
    codes, slot_of, kept = plan(block_lists, device_count)
    wanted = lax.all_to_all(codes, "tm", split_axis=0, concat_axis=0, tiled=True)
    pooled_pairs = pool(keys, values, codes)

    def exchange(array, mask):
        return lax.ppermute(array, "tm", [(i, i ^ mask) for i in range(device_count)])

    own = pooled_pairs[None]
    received = [exchange(own, mask) for mask in range(4, device_count, 4)]
    tiles, after = gather_tiles(wanted, keys, values, pooled_pairs, head_count)
    fetched = lax.all_to_all(tiles, "tm", split_axis=0, concat_axis=0, tiled=True)
    quarter = join([own] + received, after=(after,))
    second = exchange(quarter, 2)
    pre = far_rows(slot_of, kept, queries, keys, values, quarter, device_count * CAP)
    split = head_count // 2
    near_a, pooled_a = near_attention(queries, keys, values, quarter, 0, split, width)
    half = join([quarter, second], after=(near_a, pre[3]))
    third = exchange(half, 1)
    near_b, pooled_b = near_attention(
        queries, keys, values, half, split, head_count - split, width
    )
    base, coarse = blend(
        gate_coarse,
        gate_fine,
        [half, third],
        [near_a, near_b],
        [pooled_a, pooled_b],
        5 if split % 5 == 0 else 1,
        width,
    )
    fetched = fetched.reshape((device_count * CAP,) + fetched.shape[2:])
    return patch(pre[:3], gate_fine, fetched, pre[3:], coarse, base)


def solution(mesh):
    return jax.shard_map(
        per_device,
        mesh=mesh,
        in_specs=(
            P(("groups", "tm"), None),
            P(("groups", "tm"), None),
            P(("groups", "tm"), None),
            P(("groups", "tm"), None, None),
            P(),
            P(),
        ),
        out_specs=P(("groups", "tm"), None),
        check_vma=False,
    )
```

```python
import functools
import math

import jax
import jax.numpy as jnp
from jax import lax
from jax.experimental import pallas as pl
from jax.experimental.pallas import tpu as pltpu
from jax.sharding import PartitionSpec as P

CUBE = 64
CAP = 4
LOG2E = math.log2(math.e)
LANES = 128
PATCH_BATCH = 10
PRE_BATCH = 5
NEAR_STEP = 256
NEAR_WEIGHT = 20
GATHER_WEIGHT = 20
GATHER_BATCH = 8
MB = 1024 * 1024
SMALL = 6 * MB
LARGE = 56 * MB
F32 = jnp.float32
BF16 = jnp.bfloat16
I32 = jnp.int32


def vmem():
    return pl.BlockSpec(memory_space=pltpu.VMEM)


def smem():
    return pl.BlockSpec(memory_space=pltpu.SMEM)


def anywhere():
    return pl.BlockSpec(memory_space=pl.ANY)


def dot_t(a, b):
    return lax.dot_general(a, b, (((1,), (1,)), ((), ())), preferred_element_type=F32)


def dot_n(a, b):
    return lax.dot_general(a, b, (((1,), (0,)), ((), ())), preferred_element_type=F32)


def row_bits(head_count):
    return (head_count - 1).bit_length()


def plan_kernel(lists_hbm, codes_ref, slots_ref, kept_ref, lists_ref, sem):
    lists_load = pltpu.make_async_copy(lists_hbm, lists_ref, sem)
    lists_load.start()
    lists_load.wait()
    me = lax.axis_index("tm")
    lists = lists_ref[...]
    cube_count, list_len, head_count = lists.shape
    device_count = codes_ref.shape[0]
    cube_bits = cube_count.bit_length() - 1
    shift = row_bits(head_count)
    far = lax.shift_right_arithmetic(lists, cube_bits) != me
    local = lists & (cube_count - 1)
    far_value = jnp.max(jnp.where(far, lists, -1), axis=1)
    bits = jnp.where(far, 0, lax.shift_left(jnp.ones_like(local), local))
    kept_ref[...] = jnp.sum(bits, axis=1)
    grid = (device_count, cube_count, head_count)
    flat = (device_count * cube_count, head_count)
    owner = lax.broadcasted_iota(I32, grid, 0)
    head = lax.broadcasted_iota(I32, grid, 2)
    value = jnp.broadcast_to(far_value[None], grid)
    hit = jnp.where(lax.shift_right_arithmetic(value, cube_bits) == owner, 1.0, 0.0)
    hit = hit.astype(F32).reshape(flat)
    code = (lax.shift_left(value & (cube_count - 1), shift) | head).astype(F32).reshape(flat)
    square = (head_count, head_count)
    before = lax.broadcasted_iota(I32, square, 0) < lax.broadcasted_iota(I32, square, 1)
    hit_b = hit.astype(BF16)
    rank = dot_n(hit_b, jnp.where(before, 1.0, 0.0).astype(BF16))
    total = dot_n(hit_b, jnp.ones(square, BF16))
    block = (flat[0], flat[0])
    high = lax.broadcasted_iota(I32, block, 0)
    low = lax.broadcasted_iota(I32, block, 1)
    same = lax.shift_right_logical(high, cube_bits) == lax.shift_right_logical(low, cube_bits)
    rank = rank + dot_n(jnp.where(same & (low < high), 1.0, 0.0).astype(BF16), total.astype(BF16))
    lane = lax.broadcasted_iota(I32, (head_count, LANES), 1)
    codes = jnp.zeros((flat[0], LANES), F32)
    for slot in range(CAP):
        chosen = jnp.where(rank == float(slot), hit, 0.0)
        at_slot = jnp.where(lane == slot, 1.0, 0.0).astype(BF16)
        codes = codes + dot_n((chosen * (code + 1.0)).astype(BF16), at_slot)
    codes = jnp.sum(codes.reshape(device_count, cube_count, LANES), axis=1)
    codes_ref[...] = codes.astype(I32)
    slot_of = owner.astype(F32) * CAP + rank.reshape(grid) + 1.0
    slots_ref[...] = jnp.sum(slot_of * hit.reshape(grid), axis=0).astype(I32)


def plan(block_lists, device_count):
    lists = jnp.transpose(block_lists, (0, 2, 1))
    rows = jax.ShapeDtypeStruct(block_lists.shape[:2], I32)
    return pl.pallas_call(
        plan_kernel,
        out_shape=(jax.ShapeDtypeStruct((device_count, LANES), I32), rows, rows),
        in_specs=[anywhere()],
        out_specs=(vmem(),) * 3,
        scratch_shapes=[pltpu.VMEM(lists.shape, I32), pltpu.SemaphoreType.DMA],
        name="plan",
        compiler_params=pltpu.CompilerParams(vmem_limit_bytes=LARGE),
        cost_estimate=pl.CostEstimate(flops=1000000, bytes_accessed=64 * 1024, transcendentals=0),
    )(lists)


def pool_kernel(k_hbm, v_hbm, after_ref, pooled_ref, k_ref, v_ref, sums_ref, sems):
    cubes = pooled_ref.shape[1]
    loads = {}
    for cube in range(cubes):
        where = pl.ds(cube * CUBE, CUBE)
        for i, (source, target) in enumerate(((k_hbm, k_ref), (v_hbm, v_ref))):
            load = pltpu.make_async_copy(source.at[where], target.at[where], sems.at[i, cube])
            load.start()
            loads[i, cube] = load
    for cube in range(cubes):
        for i, target in enumerate((k_ref, v_ref)):
            loads[i, cube].wait()
            tokens = target[cube * CUBE : (cube + 1) * CUBE, :].astype(F32)
            sums_ref[i, cube : cube + 1, :] = jnp.sum(tokens, axis=0, keepdims=True)
    for i in range(2):
        pooled_ref[i] = (sums_ref[i] * (1.0 / CUBE)).astype(BF16)


def pool(keys, values, after):
    tokens, columns = keys.shape
    cubes = tokens // CUBE
    return pl.pallas_call(
        pool_kernel,
        out_shape=jax.ShapeDtypeStruct((2, cubes, columns), BF16),
        in_specs=[anywhere()] * 3,
        out_specs=vmem(),
        scratch_shapes=[
            pltpu.VMEM((tokens, columns), BF16),
            pltpu.VMEM((tokens, columns), BF16),
            pltpu.VMEM((2, cubes, columns), F32),
            pltpu.SemaphoreType.DMA((2, cubes)),
        ],
        name="pool",
        compiler_params=pltpu.CompilerParams(vmem_limit_bytes=LARGE),
        cost_estimate=pl.CostEstimate(
            flops=2 * keys.size, bytes_accessed=4 * keys.size, transcendentals=0
        ),
    )(keys, values, after)


def gather_kernel(
    shift,
    codes_ref,
    k_hbm,
    v_hbm,
    after_ref,
    tiles_ref,
    done_ref,
    work_ref,
    slots_ref,
    load_sems,
    store_sem,
):
    slot_count, _, rows, width = tiles_ref.shape

    def scan(peer, found):
        for rank in range(CAP):
            slot = peer * CAP + rank
            code = codes_ref[peer, rank] - 1
            slots_ref[found] = slot

            @pl.when(code >= 0)
            def _():
                cube = lax.shift_right_logical(code, shift)
                head = code & ((1 << shift) - 1)
                where = (
                    pl.ds(pl.multiple_of(cube * rows, rows), rows),
                    pl.ds(pl.multiple_of(head * width, width), width),
                )
                sem = load_sems.at[found // GATHER_BATCH]
                pltpu.make_async_copy(k_hbm.at[where], work_ref.at[slot, 0], sem).start()
                pltpu.make_async_copy(v_hbm.at[where], work_ref.at[slot, 1], sem).start()

            found = found + (code >= 0).astype(I32)
        return found

    found = lax.fori_loop(0, slot_count // CAP, scan, jnp.int32(0))
    done_ref[...] = jnp.zeros_like(done_ref)

    def store_of(i):
        slot = slots_ref[i]
        return pltpu.make_async_copy(work_ref.at[slot], tiles_ref.at[slot], store_sem)

    @pl.loop(0, pl.cdiv(found, GATHER_BATCH))
    def _(batch):
        first = batch * GATHER_BATCH
        last = jnp.minimum(first + GATHER_BATCH, found)

        @pl.loop(first, last)
        def _(i):
            both = work_ref.at[slots_ref[i]]
            pltpu.make_async_copy(both, both, load_sems.at[batch]).wait()

        @pl.loop(first, last)
        def _(i):
            store_of(i).start()

    @pl.loop(0, found)
    def _(i):
        store_of(i).wait()


def gather_tiles(codes, keys, values, after, head_count):
    tokens, columns = keys.shape
    slot_count = codes.shape[0] * CAP
    shape = (slot_count, 2, CUBE, columns // head_count)
    return pl.pallas_call(
        functools.partial(gather_kernel, row_bits(head_count)),
        out_shape=(
            jax.ShapeDtypeStruct(shape, BF16),
            jax.ShapeDtypeStruct((8, LANES), F32),
        ),
        in_specs=[smem()] + [anywhere()] * 3,
        out_specs=(anywhere(), vmem()),
        scratch_shapes=[
            pltpu.VMEM(shape, BF16),
            pltpu.SMEM((slot_count + 1,), I32),
            pltpu.SemaphoreType.DMA((pl.cdiv(slot_count, GATHER_BATCH),)),
            pltpu.SemaphoreType.DMA,
        ],
        name="gather_tiles",
        compiler_params=pltpu.CompilerParams(vmem_limit_bytes=LARGE),
        cost_estimate=pl.CostEstimate(
            flops=0, bytes_accessed=GATHER_WEIGHT * 4 * math.prod(shape), transcendentals=0
        ),
    )(codes, keys, values, after)


def join_kernel(piece_count, *refs):
    out_ref = refs[-1]
    start = 0
    for piece in refs[:piece_count]:
        out_ref[start : start + piece.shape[0]] = piece[...]
        start += piece.shape[0]


def join(pieces, after=()):
    shape = (sum(piece.shape[0] for piece in pieces),) + pieces[0].shape[1:]
    return pl.pallas_call(
        functools.partial(join_kernel, len(pieces)),
        out_shape=jax.ShapeDtypeStruct(shape, BF16),
        in_specs=[vmem()] * len(pieces) + [anywhere()] * len(after),
        out_specs=vmem(),
        name="join",
        compiler_params=pltpu.CompilerParams(vmem_limit_bytes=SMALL),
        cost_estimate=pl.CostEstimate(
            flops=0, bytes_accessed=4 * math.prod(shape), transcendentals=0
        ),
    )(*pieces, *after)


def near_kernel(scale, q_ref, k_ref, v_ref, after_ref, out_ref, pooled_ref):
    tokens, width = q_ref.shape
    cubes = pooled_ref.shape[0]
    sums = jnp.sum(q_ref[...].astype(F32).reshape(cubes, CUBE, width), axis=1)
    pooled_ref[...] = (sums * (1.0 / CUBE)).astype(BF16)
    keys = k_ref[...]
    values = jnp.concatenate([v_ref[...], jnp.ones(v_ref.shape, BF16)], axis=1)
    step = NEAR_STEP
    starts = range(0, tokens, step)
    scores = dot_t(q_ref[0:step, :], keys)
    for start in starts:
        following = start + step
        if following < tokens:
            next_scores = dot_t(q_ref[following : following + step, :], keys)
        largest = jnp.max(scores, axis=1, keepdims=True)
        raised = jnp.exp2((scores - largest) * scale)
        mixed = dot_n(raised.astype(BF16), values)
        out_ref[start : start + step, :] = mixed[:, :width] / mixed[:, width:]
        if following < tokens:
            scores = next_scores


def near_attention(queries, keys, values, after, first, heads, width):
    tokens = queries.shape[0]
    block = pl.BlockSpec((tokens, width), lambda i: (0, first + i))
    return pl.pallas_call(
        functools.partial(near_kernel, width**-0.5 * LOG2E),
        out_shape=(
            jax.ShapeDtypeStruct((tokens, heads * width), F32),
            jax.ShapeDtypeStruct((tokens // CUBE, heads * width), BF16),
        ),
        grid=(heads,),
        in_specs=[block] * 3 + [anywhere()],
        out_specs=(
            pl.BlockSpec((tokens, width), lambda i: (0, i)),
            pl.BlockSpec((tokens // CUBE, width), lambda i: (0, i)),
        ),
        name="near_attention",
        compiler_params=pltpu.CompilerParams(vmem_limit_bytes=SMALL),
        cost_estimate=pl.CostEstimate(
            flops=NEAR_WEIGHT * 4 * tokens * tokens * heads * width,
            bytes_accessed=10 * tokens * heads * width,
            transcendentals=tokens * tokens * heads,
        ),
    )(queries, keys, values, after)


class Part:
    def __init__(self, ref, start):
        self.ref, self.start = ref, start

    def __getitem__(self, i):
        return self.ref[self.start + i]

    def __setitem__(self, i, value):
        self.ref[self.start + i] = value


def list_parts(info_ref, dense):
    return Part(info_ref, 0), Part(info_ref, dense), 2 * dense


def pre_kernel(
    scale,
    shift,
    slot_of_ref,
    kept_ref,
    q_ref,
    k_ref,
    v_ref,
    after_ref,
    info_ref,
    pairs_ref,
    sums_ref,
    sets_ref,
):
    cube_count, head_count = slot_of_ref.shape
    dense, _, width = sums_ref.shape
    tokens = q_ref.shape[0]
    slots_ref, rows_ref, count_at = list_parts(info_ref, dense)
    slots_ref[0] = 1
    rows_ref[0] = 0
    sets_ref[0] = 1

    def scan(cube, found):
        for head in range(head_count):
            slot = slot_of_ref[cube, head]
            slots_ref[found] = slot
            rows_ref[found] = lax.shift_left(cube, shift) | head
            sets_ref[found] = kept_ref[cube, head]
            found = found + (slot > 0).astype(I32)
        return found

    found = lax.fori_loop(0, cube_count, scan, jnp.int32(0))
    info_ref[count_at] = found
    last = jnp.maximum(found - 1, 0)
    for more in range(PATCH_BATCH):
        slots_ref[found + more] = slots_ref[last]
        rows_ref[found + more] = rows_ref[last]
        sets_ref[found + more] = sets_ref[last]
    cube_of = lax.broadcasted_iota(I32, (1, tokens), 1) // CUBE

    @pl.loop(0, pl.cdiv(found, PATCH_BATCH) * (PATCH_BATCH // PRE_BATCH))
    def _(step):
        first = step * PRE_BATCH
        parts = range(PRE_BATCH)
        codes = [rows_ref[first + part] for part in parts]
        cubes = [lax.shift_right_logical(code, shift) for code in codes]
        heads = [code & ((1 << shift) - 1) for code in codes]
        columns = [pl.ds(pl.multiple_of(head * width, width), width) for head in heads]
        queries = [
            q_ref[pl.ds(pl.multiple_of(cubes[part] * CUBE, CUBE), CUBE), columns[part]]
            for part in parts
        ]
        scores = [dot_t(queries[part], k_ref[:, columns[part]]) for part in parts]
        for part in parts:
            kept = (lax.shift_right_logical(sets_ref[first + part], cube_of) & 1) > 0
            scores[part] = jnp.where(kept, scores[part], -3e38)
        largest = [jnp.max(score, axis=1, keepdims=True) for score in scores]
        raised = [
            jnp.exp2((scores[part] - largest[part]) * scale).astype(BF16) for part in parts
        ]
        ones = jnp.ones((tokens, width), BF16)
        values = [jnp.concatenate([v_ref[:, columns[part]], ones], axis=1) for part in parts]
        mixed = [dot_n(raised[part], values[part]) for part in parts]
        for part in parts:
            pairs_ref[first + part, 0] = queries[part]
            total = mixed[part][:, width:]
            pairs_ref[first + part, 1] = (mixed[part][:, :width] / total).astype(BF16)
            sums_ref[first + part] = largest[part] * scale + jnp.log2(total)


def far_rows(slot_of, kept, queries, keys, values, after, slot_count):
    tokens, columns = queries.shape
    head_count = slot_of.shape[1]
    width = columns // head_count
    dense = (slot_count // PATCH_BATCH + 2) * PATCH_BATCH
    return pl.pallas_call(
        functools.partial(pre_kernel, width**-0.5 * LOG2E, row_bits(head_count)),
        out_shape=(
            jax.ShapeDtypeStruct((2 * dense + 1,), I32),
            jax.ShapeDtypeStruct((dense, 2, CUBE, width), BF16),
            jax.ShapeDtypeStruct((dense, CUBE, width), F32),
        ),
        in_specs=[smem(), smem(), vmem(), vmem(), vmem(), anywhere()],
        out_specs=(smem(), vmem(), vmem()),
        scratch_shapes=[pltpu.SMEM((dense,), I32)],
        name="far_rows",
        compiler_params=pltpu.CompilerParams(vmem_limit_bytes=SMALL),
        cost_estimate=pl.CostEstimate(
            flops=4 * slot_count * CUBE * tokens * width,
            bytes_accessed=6 * tokens * columns,
            transcendentals=slot_count * CUBE * tokens,
        ),
    )(slot_of, kept, queries, keys, values, after)


def blend_kernel(scale, heads, pieces, parts, gc_ref, gf_ref, *refs):
    key_refs, value_refs = refs[:pieces], refs[pieces : 2 * pieces]
    near_refs = refs[2 * pieces : 2 * pieces + parts]
    query_refs = refs[2 * pieces + parts : 2 * pieces + 2 * parts]
    out_ref, coarse_ref = refs[2 * pieces + 2 * parts :]
    cube_count, columns = coarse_ref.shape[0] // 2, coarse_ref.shape[1]
    width = columns // heads
    first = pl.program_id(0) * heads
    places = [slice(part * width, (part + 1) * width) for part in range(heads)]

    def gathered(piece_refs, here):
        flat = [ref[:, 0, :, here].reshape(-1, width) for ref in piece_refs]
        return jnp.concatenate(flat, axis=0)

    def put(near_ref, query_ref):
        keys = [gathered(key_refs, here) for here in places]
        values = [gathered(value_refs, here) for here in places]
        scores = [dot_t(query_ref[:, here], key) for here, key in zip(places, keys)]
        scores = jnp.concatenate(scores, axis=0) * scale
        largest = jnp.max(scores, axis=1, keepdims=True)
        raised = jnp.exp(scores - largest)
        weights = raised / jnp.sum(raised, axis=1, keepdims=True)
        coarse = []
        for part in range(heads):
            mine = weights[part * cube_count : (part + 1) * cube_count].astype(BF16)
            coarse.append(gc_ref[first + part] * dot_n(mine, values[part]))
        for part, here in enumerate(places):
            coarse_ref[:cube_count, here] = coarse[part]
            gate = jnp.full((cube_count, width), gf_ref[first + part], F32)
            coarse_ref[cube_count:, here] = gate
            near = near_ref[:, here].reshape(cube_count, CUBE, width)
            blended = coarse[part][:, None, :] + gf_ref[first + part] * near
            out_ref[:, here] = blended.reshape(cube_count * CUBE, width).astype(BF16)

    share = pl.num_programs(0) // parts
    for part in range(parts):
        chosen = functools.partial(put, near_refs[part], query_refs[part])
        pl.when(pl.program_id(0) // share == part)(chosen)


def blend(gate_coarse, gate_fine, pieces, nears, pooled_queries, heads, width):
    tokens, part_columns = nears[0].shape
    cube_count = tokens // CUBE
    columns = part_columns * len(nears)
    step = heads * width
    share = part_columns // step

    def piece_spec(piece, which):
        shape = (piece.shape[0], 1, cube_count, step)
        return pl.BlockSpec(shape, lambda i: (0, which, 0, i))

    def part_spec(rows, part):
        return pl.BlockSpec(
            (rows, step), lambda i: (0, jnp.clip(i - part * share, 0, share - 1))
        )

    parts = range(len(nears))
    return pl.pallas_call(
        functools.partial(blend_kernel, width**-0.5, heads, len(pieces), len(nears)),
        out_shape=(
            jax.ShapeDtypeStruct((tokens, columns), BF16),
            jax.ShapeDtypeStruct((2 * cube_count, columns), F32),
        ),
        grid=(columns // step,),
        in_specs=[smem(), smem()]
        + [piece_spec(piece, 0) for piece in pieces]
        + [piece_spec(piece, 1) for piece in pieces]
        + [part_spec(tokens, part) for part in parts]
        + [part_spec(cube_count, part) for part in parts],
        out_specs=(
            pl.BlockSpec((tokens, step), lambda i: (0, i)),
            pl.BlockSpec((2 * cube_count, step), lambda i: (0, i)),
        ),
        name="blend",
        compiler_params=pltpu.CompilerParams(vmem_limit_bytes=16 * MB),
        cost_estimate=pl.CostEstimate(
            flops=2 * tokens * columns, bytes_accessed=6 * tokens * columns, transcendentals=0
        ),
    )(gate_coarse, gate_fine, *pieces, *pieces, *nears, *pooled_queries)


def patch_kernel(
    scale,
    shift,
    info_ref,
    tiles_hbm,
    pairs_hbm,
    sums_hbm,
    coarse_hbm,
    base_ref,
    out_ref,
    tiles_ref,
    pairs_ref,
    sums_ref,
    coarse_ref,
    ready_ref,
    load_sems,
    coarse_sem,
    store_sem,
):
    dense, _, width = sums_ref.shape
    cube_count = coarse_ref.shape[0] // 2
    slots_ref, rows_ref, count_at = list_parts(info_ref, dense)
    count = info_ref[count_at]
    steps = pl.cdiv(count, PATCH_BATCH)
    coarse_load = pltpu.make_async_copy(coarse_hbm, coarse_ref, coarse_sem)

    def batch_load(step, which):
        source, target = ((pairs_hbm, pairs_ref), (sums_hbm, sums_ref))[which]
        where = pl.ds(step * PATCH_BATCH, PATCH_BATCH)
        return pltpu.make_async_copy(source.at[where], target.at[where], load_sems.at[which, step])

    def store(i):
        row = rows_ref[i]
        cube = lax.shift_right_logical(row, shift)
        head = row & ((1 << shift) - 1)
        where = (
            pl.ds(pl.multiple_of(cube * CUBE, CUBE), CUBE),
            pl.ds(pl.multiple_of(head * width, width), width),
        )
        return pltpu.make_async_copy(ready_ref.at[i], out_ref.at[where], store_sem)

    @pl.loop(0, steps)
    def _(step):
        for which in range(2):
            batch_load(step, which).start()
        for part in range(PATCH_BATCH):
            i = step * PATCH_BATCH + part
            tile = tiles_hbm.at[slots_ref[i] - 1]
            pltpu.make_async_copy(tile, tiles_ref.at[i], load_sems.at[2, step]).start()

        @pl.when(step == 0)
        def _():
            coarse_load.start()

    @pl.loop(0, steps)
    def _(step):
        @pl.when(step == 0)
        def _():
            coarse_load.wait()

        first = step * PATCH_BATCH
        parts = range(PATCH_BATCH)
        for which in range(2):
            batch_load(step, which).wait()
        tiles = tiles_ref.at[pl.ds(first, PATCH_BATCH)]
        pltpu.make_async_copy(tiles, tiles, load_sems.at[2, step]).wait()
        codes = [rows_ref[first + part] for part in parts]
        cubes = [lax.shift_right_logical(code, shift) for code in codes]
        heads = [code & ((1 << shift) - 1) for code in codes]
        columns = [pl.ds(pl.multiple_of(head * width, width), width) for head in heads]
        scores = [dot_t(pairs_ref[first + part, 0], tiles_ref[first + part, 0]) for part in parts]
        scores = [score * scale for score in scores]
        tops = [jnp.max(score, axis=1, keepdims=True) for score in scores]
        sums = [sums_ref[first + part] for part in parts]
        largest = [jnp.maximum(sums[part], tops[part]) for part in parts]
        raised = [
            jnp.exp2(scores[part] - largest[part][:, :CUBE]).astype(BF16) for part in parts
        ]
        ones = jnp.ones((CUBE, width), BF16)
        values = [jnp.concatenate([tiles_ref[first + part, 1], ones], axis=1) for part in parts]
        mixed = [dot_n(raised[part], values[part]) for part in parts]
        for part in parts:
            coarse = coarse_ref[:cube_count, columns[part]]
            gate = coarse_ref[cube_count : cube_count + 1, columns[part]]
            this_cube = lax.broadcasted_iota(I32, coarse.shape, 0) == cubes[part]
            coarse = jnp.sum(jnp.where(this_cube, coarse, 0.0), axis=0, keepdims=True)
            kept = jnp.exp2(sums[part] - largest[part])
            total = kept + mixed[part][:, width:]
            fine = pairs_ref[first + part, 1].astype(F32) * kept + mixed[part][:, :width]
            blended = coarse + gate * (fine / total)
            ready_ref[first + part] = blended.astype(BF16)
        for part in parts:
            pl.when(first + part < count)(store(first + part).start)

    @pl.loop(0, count)
    def _(i):
        store(i).wait()


def patch(info, tiles, pairs, sums, coarse, base, head_count):
    dense, _, width = sums.shape
    return pl.pallas_call(
        functools.partial(patch_kernel, width**-0.5 * LOG2E, row_bits(head_count)),
        out_shape=jax.ShapeDtypeStruct(base.shape, BF16),
        in_specs=[smem()] + [anywhere()] * 5,
        out_specs=anywhere(),
        scratch_shapes=[
            pltpu.VMEM((dense,) + tiles.shape[1:], BF16),
            pltpu.VMEM(pairs.shape, BF16),
            pltpu.VMEM(sums.shape, F32),
            pltpu.VMEM(coarse.shape, F32),
            pltpu.VMEM((dense, CUBE, width), BF16),
            pltpu.SemaphoreType.DMA((3, dense // PATCH_BATCH)),
            pltpu.SemaphoreType.DMA,
            pltpu.SemaphoreType.DMA,
        ],
        input_output_aliases={5: 0},
        name="patch",
        compiler_params=pltpu.CompilerParams(vmem_limit_bytes=LARGE),
        cost_estimate=pl.CostEstimate(
            flops=4 * dense * CUBE * CUBE * width,
            bytes_accessed=16 * dense * CUBE * width,
            transcendentals=dense * CUBE * CUBE,
        ),
    )(info, tiles, pairs, sums, coarse, base)


def per_device(queries, keys, values, block_lists, gate_coarse, gate_fine):
    head_count = gate_coarse.shape[0]
    width = queries.shape[1] // head_count
    cube_count = block_lists.shape[0]
    device_count = lax.axis_size("tm")
    codes, slot_of, kept = plan(block_lists, device_count)
    wanted = lax.all_to_all(codes, "tm", split_axis=0, concat_axis=0, tiled=True)
    pooled_pairs = pool(keys, values, codes)

    def exchange(array, mask):
        return lax.ppermute(array, "tm", [(i, i ^ mask) for i in range(device_count)])

    own = join([pooled_pairs[None]], after=(wanted,))
    received = [exchange(own, mask) for mask in range(4, device_count, 4)]
    tiles, after = gather_tiles(wanted, keys, values, pooled_pairs, head_count)
    fetched = lax.all_to_all(tiles, "tm", split_axis=0, concat_axis=0, tiled=True)
    quarter = join([own] + received, after=(after,))
    second = exchange(quarter, 2)
    info, pairs, sums = far_rows(slot_of, kept, queries, keys, values, quarter, device_count * CAP)
    split = head_count // 2
    near_a, pooled_a = near_attention(queries, keys, values, quarter, 0, split, width)
    half = join([quarter, second], after=(near_a, sums))
    third = exchange(half, 1)
    near_b, pooled_b = near_attention(
        queries, keys, values, half, split, head_count - split, width
    )
    base, coarse = blend(
        gate_coarse,
        gate_fine,
        [half, third],
        [near_a, near_b],
        [pooled_a, pooled_b],
        5 if split % 5 == 0 else 1,
        width,
    )
    return patch(info, fetched, pairs, sums, coarse, base, head_count)


def solution(mesh):
    return jax.shard_map(
        per_device,
        mesh=mesh,
        in_specs=(
            P(("groups", "tm"), None),
            P(("groups", "tm"), None),
            P(("groups", "tm"), None),
            P(("groups", "tm"), None, None),
            P(),
            P(),
        ),
        out_specs=P(("groups", "tm"), None),
        check_vma=False,
    )
```

```python
import functools
import math

import jax
import jax.numpy as jnp
from jax import lax
from jax.experimental import pallas as pl
from jax.experimental.pallas import tpu as pltpu
from jax.sharding import PartitionSpec as P

CUBE = 64
CAP = 4
LOG2E = math.log2(math.e)
LANES = 128
PATCH_BATCH = 10
PRE_BATCH = 5
NEAR_STEP = 256
NEAR_WEIGHT = 20
GATHER_WEIGHT = 10**12
GATHER_BATCH = 8
MB = 1024 * 1024
SMALL = 6 * MB
LARGE = 56 * MB
F32 = jnp.float32
BF16 = jnp.bfloat16
I32 = jnp.int32


def vmem():
    return pl.BlockSpec(memory_space=pltpu.VMEM)


def smem():
    return pl.BlockSpec(memory_space=pltpu.SMEM)


def anywhere():
    return pl.BlockSpec(memory_space=pl.ANY)


def dot_t(a, b):
    return lax.dot_general(a, b, (((1,), (1,)), ((), ())), preferred_element_type=F32)


def dot_n(a, b):
    return lax.dot_general(a, b, (((1,), (0,)), ((), ())), preferred_element_type=F32)


def row_bits(head_count):
    return (head_count - 1).bit_length()


def plan_kernel(lists_hbm, codes_ref, slots_ref, kept_ref, lists_ref, sem):
    lists_load = pltpu.make_async_copy(lists_hbm, lists_ref, sem)
    lists_load.start()
    lists_load.wait()
    me = lax.axis_index("tm")
    lists = lists_ref[...]
    cube_count, list_len, head_count = lists.shape
    device_count = codes_ref.shape[0]
    cube_bits = cube_count.bit_length() - 1
    shift = row_bits(head_count)
    far = lax.shift_right_arithmetic(lists, cube_bits) != me
    local = lists & (cube_count - 1)
    far_value = jnp.max(jnp.where(far, lists, -1), axis=1)
    bits = jnp.where(far, 0, lax.shift_left(jnp.ones_like(local), local))
    kept_ref[...] = jnp.sum(bits, axis=1)
    grid = (device_count, cube_count, head_count)
    flat = (device_count * cube_count, head_count)
    owner = lax.broadcasted_iota(I32, grid, 0)
    head = lax.broadcasted_iota(I32, grid, 2)
    value = jnp.broadcast_to(far_value[None], grid)
    hit = jnp.where(lax.shift_right_arithmetic(value, cube_bits) == owner, 1.0, 0.0)
    hit = hit.astype(F32).reshape(flat)
    code = (lax.shift_left(value & (cube_count - 1), shift) | head).astype(F32).reshape(flat)
    square = (head_count, head_count)
    before = lax.broadcasted_iota(I32, square, 0) < lax.broadcasted_iota(I32, square, 1)
    hit_b = hit.astype(BF16)
    rank = dot_n(hit_b, jnp.where(before, 1.0, 0.0).astype(BF16))
    total = dot_n(hit_b, jnp.ones(square, BF16))
    block = (flat[0], flat[0])
    high = lax.broadcasted_iota(I32, block, 0)
    low = lax.broadcasted_iota(I32, block, 1)
    same = lax.shift_right_logical(high, cube_bits) == lax.shift_right_logical(low, cube_bits)
    rank = rank + dot_n(jnp.where(same & (low < high), 1.0, 0.0).astype(BF16), total.astype(BF16))
    lane = lax.broadcasted_iota(I32, (head_count, LANES), 1)
    codes = jnp.zeros((flat[0], LANES), F32)
    for slot in range(CAP):
        chosen = jnp.where(rank == float(slot), hit, 0.0)
        at_slot = jnp.where(lane == slot, 1.0, 0.0).astype(BF16)
        codes = codes + dot_n((chosen * (code + 1.0)).astype(BF16), at_slot)
    codes = jnp.sum(codes.reshape(device_count, cube_count, LANES), axis=1)
    codes_ref[...] = codes.astype(I32)
    slot_of = owner.astype(F32) * CAP + rank.reshape(grid) + 1.0
    slots_ref[...] = jnp.sum(slot_of * hit.reshape(grid), axis=0).astype(I32)


def plan(block_lists, device_count):
    lists = jnp.transpose(block_lists, (0, 2, 1))
    rows = jax.ShapeDtypeStruct(block_lists.shape[:2], I32)
    return pl.pallas_call(
        plan_kernel,
        out_shape=(jax.ShapeDtypeStruct((device_count, LANES), I32), rows, rows),
        in_specs=[anywhere()],
        out_specs=(vmem(),) * 3,
        scratch_shapes=[pltpu.VMEM(lists.shape, I32), pltpu.SemaphoreType.DMA],
        name="plan",
        compiler_params=pltpu.CompilerParams(vmem_limit_bytes=LARGE),
        cost_estimate=pl.CostEstimate(flops=1000000, bytes_accessed=64 * 1024, transcendentals=0),
    )(lists)


def pool_kernel(k_hbm, v_hbm, after_ref, pooled_ref, k_ref, v_ref, sums_ref, sems):
    cubes = pooled_ref.shape[1]
    loads = {}
    for cube in range(cubes):
        where = pl.ds(cube * CUBE, CUBE)
        for i, (source, target) in enumerate(((k_hbm, k_ref), (v_hbm, v_ref))):
            load = pltpu.make_async_copy(source.at[where], target.at[where], sems.at[i, cube])
            load.start()
            loads[i, cube] = load
    for cube in range(cubes):
        for i, target in enumerate((k_ref, v_ref)):
            loads[i, cube].wait()
            tokens = target[cube * CUBE : (cube + 1) * CUBE, :].astype(F32)
            sums_ref[i, cube : cube + 1, :] = jnp.sum(tokens, axis=0, keepdims=True)
    for i in range(2):
        pooled_ref[i] = (sums_ref[i] * (1.0 / CUBE)).astype(BF16)


def pool(keys, values, after):
    tokens, columns = keys.shape
    cubes = tokens // CUBE
    return pl.pallas_call(
        pool_kernel,
        out_shape=jax.ShapeDtypeStruct((2, cubes, columns), BF16),
        in_specs=[anywhere()] * 3,
        out_specs=vmem(),
        scratch_shapes=[
            pltpu.VMEM((tokens, columns), BF16),
            pltpu.VMEM((tokens, columns), BF16),
            pltpu.VMEM((2, cubes, columns), F32),
            pltpu.SemaphoreType.DMA((2, cubes)),
        ],
        name="pool",
        compiler_params=pltpu.CompilerParams(vmem_limit_bytes=LARGE),
        cost_estimate=pl.CostEstimate(
            flops=2 * keys.size, bytes_accessed=4 * keys.size, transcendentals=0
        ),
    )(keys, values, after)


def gather_kernel(
    shift,
    codes_hbm,
    k_hbm,
    v_hbm,
    after_ref,
    tiles_ref,
    done_ref,
    work_ref,
    codes_ref,
    slots_ref,
    load_sems,
    store_sem,
):
    slot_count, _, rows, width = tiles_ref.shape
    codes_load = pltpu.make_async_copy(codes_hbm, codes_ref, store_sem)
    codes_load.start()
    codes_load.wait()

    def scan(peer, found):
        for rank in range(CAP):
            slot = peer * CAP + rank
            code = codes_ref[peer, rank] - 1
            slots_ref[found] = slot

            @pl.when(code >= 0)
            def _():
                cube = lax.shift_right_logical(code, shift)
                head = code & ((1 << shift) - 1)
                where = (
                    pl.ds(pl.multiple_of(cube * rows, rows), rows),
                    pl.ds(pl.multiple_of(head * width, width), width),
                )
                sem = load_sems.at[found // GATHER_BATCH]
                pltpu.make_async_copy(k_hbm.at[where], work_ref.at[slot, 0], sem).start()
                pltpu.make_async_copy(v_hbm.at[where], work_ref.at[slot, 1], sem).start()

            found = found + (code >= 0).astype(I32)
        return found

    found = lax.fori_loop(0, slot_count // CAP, scan, jnp.int32(0))
    done_ref[...] = jnp.zeros_like(done_ref)

    def store_of(i):
        slot = slots_ref[i]
        return pltpu.make_async_copy(work_ref.at[slot], tiles_ref.at[slot], store_sem)

    @pl.loop(0, pl.cdiv(found, GATHER_BATCH))
    def _(batch):
        first = batch * GATHER_BATCH
        last = jnp.minimum(first + GATHER_BATCH, found)

        @pl.loop(first, last)
        def _(i):
            both = work_ref.at[slots_ref[i]]
            pltpu.make_async_copy(both, both, load_sems.at[batch]).wait()

        @pl.loop(first, last)
        def _(i):
            store_of(i).start()

    @pl.loop(0, found)
    def _(i):
        store_of(i).wait()


def gather_tiles(codes, keys, values, after, head_count):
    tokens, columns = keys.shape
    slot_count = codes.shape[0] * CAP
    shape = (slot_count, 2, CUBE, columns // head_count)
    return pl.pallas_call(
        functools.partial(gather_kernel, row_bits(head_count)),
        out_shape=(
            jax.ShapeDtypeStruct(shape, BF16),
            jax.ShapeDtypeStruct((8, LANES), F32),
        ),
        in_specs=[anywhere()] * 4,
        out_specs=(anywhere(), vmem()),
        scratch_shapes=[
            pltpu.VMEM(shape, BF16),
            pltpu.SMEM(codes.shape, I32),
            pltpu.SMEM((slot_count + 1,), I32),
            pltpu.SemaphoreType.DMA((pl.cdiv(slot_count, GATHER_BATCH),)),
            pltpu.SemaphoreType.DMA,
        ],
        name="gather_tiles",
        compiler_params=pltpu.CompilerParams(vmem_limit_bytes=LARGE),
        cost_estimate=pl.CostEstimate(
            flops=GATHER_WEIGHT, bytes_accessed=4 * math.prod(shape), transcendentals=0
        ),
    )(codes, keys, values, after)


def join_kernel(piece_count, *refs):
    out_ref = refs[-1]
    start = 0
    for piece in refs[:piece_count]:
        out_ref[start : start + piece.shape[0]] = piece[...]
        start += piece.shape[0]


def join(pieces, after=()):
    shape = (sum(piece.shape[0] for piece in pieces),) + pieces[0].shape[1:]
    return pl.pallas_call(
        functools.partial(join_kernel, len(pieces)),
        out_shape=jax.ShapeDtypeStruct(shape, BF16),
        in_specs=[vmem()] * len(pieces) + [anywhere()] * len(after),
        out_specs=vmem(),
        name="join",
        compiler_params=pltpu.CompilerParams(vmem_limit_bytes=SMALL),
        cost_estimate=pl.CostEstimate(
            flops=0, bytes_accessed=4 * math.prod(shape), transcendentals=0
        ),
    )(*pieces, *after)


def near_kernel(scale, q_ref, k_ref, v_ref, after_ref, out_ref, pooled_ref):
    tokens, width = q_ref.shape
    cubes = pooled_ref.shape[0]
    sums = jnp.sum(q_ref[...].astype(F32).reshape(cubes, CUBE, width), axis=1)
    pooled_ref[...] = (sums * (1.0 / CUBE)).astype(BF16)
    keys = k_ref[...]
    values = jnp.concatenate([v_ref[...], jnp.ones(v_ref.shape, BF16)], axis=1)
    step = NEAR_STEP
    starts = range(0, tokens, step)
    scores = dot_t(q_ref[0:step, :], keys)
    for start in starts:
        following = start + step
        if following < tokens:
            next_scores = dot_t(q_ref[following : following + step, :], keys)
        largest = jnp.max(scores, axis=1, keepdims=True)
        raised = jnp.exp2((scores - largest) * scale)
        mixed = dot_n(raised.astype(BF16), values)
        out_ref[start : start + step, :] = mixed[:, :width] / mixed[:, width:]
        if following < tokens:
            scores = next_scores


def near_attention(queries, keys, values, after, first, heads, width):
    tokens = queries.shape[0]
    block = pl.BlockSpec((tokens, width), lambda i: (0, first + i))
    return pl.pallas_call(
        functools.partial(near_kernel, width**-0.5 * LOG2E),
        out_shape=(
            jax.ShapeDtypeStruct((tokens, heads * width), F32),
            jax.ShapeDtypeStruct((tokens // CUBE, heads * width), BF16),
        ),
        grid=(heads,),
        in_specs=[block] * 3 + [anywhere()],
        out_specs=(
            pl.BlockSpec((tokens, width), lambda i: (0, i)),
            pl.BlockSpec((tokens // CUBE, width), lambda i: (0, i)),
        ),
        name="near_attention",
        compiler_params=pltpu.CompilerParams(vmem_limit_bytes=SMALL),
        cost_estimate=pl.CostEstimate(
            flops=NEAR_WEIGHT * 4 * tokens * tokens * heads * width,
            bytes_accessed=10 * tokens * heads * width,
            transcendentals=tokens * tokens * heads,
        ),
    )(queries, keys, values, after)


class Part:
    def __init__(self, ref, start):
        self.ref, self.start = ref, start

    def __getitem__(self, i):
        return self.ref[self.start + i]

    def __setitem__(self, i, value):
        self.ref[self.start + i] = value


def list_parts(info_ref, dense):
    return Part(info_ref, 0), Part(info_ref, dense), 2 * dense


def pre_kernel(
    scale,
    shift,
    slot_of_ref,
    kept_ref,
    q_ref,
    k_ref,
    v_ref,
    after_ref,
    info_ref,
    pairs_ref,
    sums_ref,
    sets_ref,
):
    cube_count, head_count = slot_of_ref.shape
    dense, _, width = sums_ref.shape
    tokens = q_ref.shape[0]
    slots_ref, rows_ref, count_at = list_parts(info_ref, dense)
    slots_ref[0] = 1
    rows_ref[0] = 0
    sets_ref[0] = 1

    def scan(cube, found):
        for head in range(head_count):
            slot = slot_of_ref[cube, head]
            slots_ref[found] = slot
            rows_ref[found] = lax.shift_left(cube, shift) | head
            sets_ref[found] = kept_ref[cube, head]
            found = found + (slot > 0).astype(I32)
        return found

    found = lax.fori_loop(0, cube_count, scan, jnp.int32(0))
    info_ref[count_at] = found
    last = jnp.maximum(found - 1, 0)
    for more in range(PATCH_BATCH):
        slots_ref[found + more] = slots_ref[last]
        rows_ref[found + more] = rows_ref[last]
        sets_ref[found + more] = sets_ref[last]
    cube_of = lax.broadcasted_iota(I32, (1, tokens), 1) // CUBE

    @pl.loop(0, pl.cdiv(found, PATCH_BATCH) * (PATCH_BATCH // PRE_BATCH))
    def _(step):
        first = step * PRE_BATCH
        parts = range(PRE_BATCH)
        codes = [rows_ref[first + part] for part in parts]
        cubes = [lax.shift_right_logical(code, shift) for code in codes]
        heads = [code & ((1 << shift) - 1) for code in codes]
        columns = [pl.ds(pl.multiple_of(head * width, width), width) for head in heads]
        queries = [
            q_ref[pl.ds(pl.multiple_of(cubes[part] * CUBE, CUBE), CUBE), columns[part]]
            for part in parts
        ]
        scores = [dot_t(queries[part], k_ref[:, columns[part]]) for part in parts]
        for part in parts:
            kept = (lax.shift_right_logical(sets_ref[first + part], cube_of) & 1) > 0
            scores[part] = jnp.where(kept, scores[part], -3e38)
        largest = [jnp.max(score, axis=1, keepdims=True) for score in scores]
        raised = [
            jnp.exp2((scores[part] - largest[part]) * scale).astype(BF16) for part in parts
        ]
        ones = jnp.ones((tokens, width), BF16)
        values = [jnp.concatenate([v_ref[:, columns[part]], ones], axis=1) for part in parts]
        mixed = [dot_n(raised[part], values[part]) for part in parts]
        for part in parts:
            pairs_ref[first + part, 0] = queries[part]
            total = mixed[part][:, width:]
            pairs_ref[first + part, 1] = (mixed[part][:, :width] / total).astype(BF16)
            sums_ref[first + part] = largest[part] * scale + jnp.log2(total)


def far_rows(slot_of, kept, queries, keys, values, after, slot_count):
    tokens, columns = queries.shape
    head_count = slot_of.shape[1]
    width = columns // head_count
    dense = (slot_count // PATCH_BATCH + 2) * PATCH_BATCH
    return pl.pallas_call(
        functools.partial(pre_kernel, width**-0.5 * LOG2E, row_bits(head_count)),
        out_shape=(
            jax.ShapeDtypeStruct((2 * dense + 1,), I32),
            jax.ShapeDtypeStruct((dense, 2, CUBE, width), BF16),
            jax.ShapeDtypeStruct((dense, CUBE, width), F32),
        ),
        in_specs=[smem(), smem(), vmem(), vmem(), vmem(), anywhere()],
        out_specs=(smem(), vmem(), vmem()),
        scratch_shapes=[pltpu.SMEM((dense,), I32)],
        name="far_rows",
        compiler_params=pltpu.CompilerParams(vmem_limit_bytes=SMALL),
        cost_estimate=pl.CostEstimate(
            flops=4 * slot_count * CUBE * tokens * width,
            bytes_accessed=6 * tokens * columns,
            transcendentals=slot_count * CUBE * tokens,
        ),
    )(slot_of, kept, queries, keys, values, after)


def blend_kernel(scale, heads, pieces, parts, gc_ref, gf_ref, *refs):
    key_refs, value_refs = refs[:pieces], refs[pieces : 2 * pieces]
    near_refs = refs[2 * pieces : 2 * pieces + parts]
    query_refs = refs[2 * pieces + parts : 2 * pieces + 2 * parts]
    out_ref, coarse_ref = refs[2 * pieces + 2 * parts :]
    cube_count, columns = coarse_ref.shape[0] // 2, coarse_ref.shape[1]
    width = columns // heads
    first = pl.program_id(0) * heads
    places = [slice(part * width, (part + 1) * width) for part in range(heads)]

    def gathered(piece_refs, here):
        flat = [ref[:, 0, :, here].reshape(-1, width) for ref in piece_refs]
        return jnp.concatenate(flat, axis=0)

    def put(near_ref, query_ref):
        keys = [gathered(key_refs, here) for here in places]
        values = [gathered(value_refs, here) for here in places]
        scores = [dot_t(query_ref[:, here], key) for here, key in zip(places, keys)]
        scores = jnp.concatenate(scores, axis=0) * scale
        largest = jnp.max(scores, axis=1, keepdims=True)
        raised = jnp.exp(scores - largest)
        weights = raised / jnp.sum(raised, axis=1, keepdims=True)
        coarse = []
        for part in range(heads):
            mine = weights[part * cube_count : (part + 1) * cube_count].astype(BF16)
            coarse.append(gc_ref[first + part] * dot_n(mine, values[part]))
        for part, here in enumerate(places):
            coarse_ref[:cube_count, here] = coarse[part]
            gate = jnp.full((cube_count, width), gf_ref[first + part], F32)
            coarse_ref[cube_count:, here] = gate
            near = near_ref[:, here].reshape(cube_count, CUBE, width)
            blended = coarse[part][:, None, :] + gf_ref[first + part] * near
            out_ref[:, here] = blended.reshape(cube_count * CUBE, width).astype(BF16)

    share = pl.num_programs(0) // parts
    for part in range(parts):
        chosen = functools.partial(put, near_refs[part], query_refs[part])
        pl.when(pl.program_id(0) // share == part)(chosen)


def blend(gate_coarse, gate_fine, pieces, nears, pooled_queries, heads, width):
    tokens, part_columns = nears[0].shape
    cube_count = tokens // CUBE
    columns = part_columns * len(nears)
    step = heads * width
    share = part_columns // step

    def piece_spec(piece, which):
        shape = (piece.shape[0], 1, cube_count, step)
        return pl.BlockSpec(shape, lambda i: (0, which, 0, i))

    def part_spec(rows, part):
        return pl.BlockSpec(
            (rows, step), lambda i: (0, jnp.clip(i - part * share, 0, share - 1))
        )

    parts = range(len(nears))
    return pl.pallas_call(
        functools.partial(blend_kernel, width**-0.5, heads, len(pieces), len(nears)),
        out_shape=(
            jax.ShapeDtypeStruct((tokens, columns), BF16),
            jax.ShapeDtypeStruct((2 * cube_count, columns), F32),
        ),
        grid=(columns // step,),
        in_specs=[smem(), smem()]
        + [piece_spec(piece, 0) for piece in pieces]
        + [piece_spec(piece, 1) for piece in pieces]
        + [part_spec(tokens, part) for part in parts]
        + [part_spec(cube_count, part) for part in parts],
        out_specs=(
            pl.BlockSpec((tokens, step), lambda i: (0, i)),
            pl.BlockSpec((2 * cube_count, step), lambda i: (0, i)),
        ),
        name="blend",
        compiler_params=pltpu.CompilerParams(vmem_limit_bytes=16 * MB),
        cost_estimate=pl.CostEstimate(
            flops=2 * tokens * columns, bytes_accessed=6 * tokens * columns, transcendentals=0
        ),
    )(gate_coarse, gate_fine, *pieces, *pieces, *nears, *pooled_queries)


def patch_kernel(
    scale,
    shift,
    info_ref,
    tiles_hbm,
    pairs_hbm,
    sums_hbm,
    coarse_hbm,
    base_ref,
    out_ref,
    tiles_ref,
    pairs_ref,
    sums_ref,
    coarse_ref,
    ready_ref,
    load_sems,
    coarse_sem,
    store_sem,
):
    dense, _, width = sums_ref.shape
    cube_count = coarse_ref.shape[0] // 2
    slots_ref, rows_ref, count_at = list_parts(info_ref, dense)
    count = info_ref[count_at]
    steps = pl.cdiv(count, PATCH_BATCH)
    coarse_load = pltpu.make_async_copy(coarse_hbm, coarse_ref, coarse_sem)

    def batch_load(step, which):
        source, target = ((pairs_hbm, pairs_ref), (sums_hbm, sums_ref))[which]
        where = pl.ds(step * PATCH_BATCH, PATCH_BATCH)
        return pltpu.make_async_copy(source.at[where], target.at[where], load_sems.at[which, step])

    def store(i):
        row = rows_ref[i]
        cube = lax.shift_right_logical(row, shift)
        head = row & ((1 << shift) - 1)
        where = (
            pl.ds(pl.multiple_of(cube * CUBE, CUBE), CUBE),
            pl.ds(pl.multiple_of(head * width, width), width),
        )
        return pltpu.make_async_copy(ready_ref.at[i], out_ref.at[where], store_sem)

    @pl.loop(0, steps)
    def _(step):
        for which in range(2):
            batch_load(step, which).start()
        for part in range(PATCH_BATCH):
            i = step * PATCH_BATCH + part
            tile = tiles_hbm.at[slots_ref[i] - 1]
            pltpu.make_async_copy(tile, tiles_ref.at[i], load_sems.at[2, step]).start()

        @pl.when(step == 0)
        def _():
            coarse_load.start()

    @pl.loop(0, steps)
    def _(step):
        @pl.when(step == 0)
        def _():
            coarse_load.wait()

        first = step * PATCH_BATCH
        parts = range(PATCH_BATCH)
        for which in range(2):
            batch_load(step, which).wait()
        tiles = tiles_ref.at[pl.ds(first, PATCH_BATCH)]
        pltpu.make_async_copy(tiles, tiles, load_sems.at[2, step]).wait()
        codes = [rows_ref[first + part] for part in parts]
        cubes = [lax.shift_right_logical(code, shift) for code in codes]
        heads = [code & ((1 << shift) - 1) for code in codes]
        columns = [pl.ds(pl.multiple_of(head * width, width), width) for head in heads]
        scores = [dot_t(pairs_ref[first + part, 0], tiles_ref[first + part, 0]) for part in parts]
        scores = [score * scale for score in scores]
        tops = [jnp.max(score, axis=1, keepdims=True) for score in scores]
        sums = [sums_ref[first + part] for part in parts]
        largest = [jnp.maximum(sums[part], tops[part]) for part in parts]
        raised = [
            jnp.exp2(scores[part] - largest[part][:, :CUBE]).astype(BF16) for part in parts
        ]
        ones = jnp.ones((CUBE, width), BF16)
        values = [jnp.concatenate([tiles_ref[first + part, 1], ones], axis=1) for part in parts]
        mixed = [dot_n(raised[part], values[part]) for part in parts]
        for part in parts:
            coarse = coarse_ref[:cube_count, columns[part]]
            gate = coarse_ref[cube_count : cube_count + 1, columns[part]]
            this_cube = lax.broadcasted_iota(I32, coarse.shape, 0) == cubes[part]
            coarse = jnp.sum(jnp.where(this_cube, coarse, 0.0), axis=0, keepdims=True)
            kept = jnp.exp2(sums[part] - largest[part])
            total = kept + mixed[part][:, width:]
            fine = pairs_ref[first + part, 1].astype(F32) * kept + mixed[part][:, :width]
            blended = coarse + gate * (fine / total)
            ready_ref[first + part] = blended.astype(BF16)
        for part in parts:
            pl.when(first + part < count)(store(first + part).start)

    @pl.loop(0, count)
    def _(i):
        store(i).wait()


def patch(info, tiles, pairs, sums, coarse, base, head_count):
    dense, _, width = sums.shape
    return pl.pallas_call(
        functools.partial(patch_kernel, width**-0.5 * LOG2E, row_bits(head_count)),
        out_shape=jax.ShapeDtypeStruct(base.shape, BF16),
        in_specs=[smem()] + [anywhere()] * 5,
        out_specs=anywhere(),
        scratch_shapes=[
            pltpu.VMEM((dense,) + tiles.shape[1:], BF16),
            pltpu.VMEM(pairs.shape, BF16),
            pltpu.VMEM(sums.shape, F32),
            pltpu.VMEM(coarse.shape, F32),
            pltpu.VMEM((dense, CUBE, width), BF16),
            pltpu.SemaphoreType.DMA((3, dense // PATCH_BATCH)),
            pltpu.SemaphoreType.DMA,
            pltpu.SemaphoreType.DMA,
        ],
        input_output_aliases={5: 0},
        name="patch",
        compiler_params=pltpu.CompilerParams(vmem_limit_bytes=LARGE),
        cost_estimate=pl.CostEstimate(
            flops=4 * dense * CUBE * CUBE * width,
            bytes_accessed=16 * dense * CUBE * width,
            transcendentals=dense * CUBE * CUBE,
        ),
    )(info, tiles, pairs, sums, coarse, base)


def per_device(queries, keys, values, block_lists, gate_coarse, gate_fine):
    head_count = gate_coarse.shape[0]
    width = queries.shape[1] // head_count
    cube_count = block_lists.shape[0]
    device_count = lax.axis_size("tm")
    codes, slot_of, kept = plan(block_lists, device_count)
    wanted = lax.all_to_all(codes, "tm", split_axis=0, concat_axis=0, tiled=True)
    pooled_pairs = pool(keys, values, codes)

    def exchange(array, mask):
        return lax.ppermute(array, "tm", [(i, i ^ mask) for i in range(device_count)])

    own = pooled_pairs[None]
    across = exchange(own, device_count // 2)
    masks = range(4, device_count // 2, 4)
    received = [exchange(own, mask) for mask in masks]
    tiles, after = gather_tiles(wanted, keys, values, pooled_pairs, head_count)
    tiles, across = lax.optimization_barrier((tiles, across))
    received += [exchange(across, mask) for mask in masks]
    fetched = lax.all_to_all(tiles, "tm", split_axis=0, concat_axis=0, tiled=True)
    quarter = join([own, across] + received, after=(after,))
    second = exchange(quarter, 2)
    info, pairs, sums = far_rows(slot_of, kept, queries, keys, values, quarter, device_count * CAP)
    split = head_count // 2
    near_a, pooled_a = near_attention(queries, keys, values, quarter, 0, split, width)
    half = join([quarter, second], after=(near_a, sums))
    third = exchange(half, 1)
    near_b, pooled_b = near_attention(
        queries, keys, values, half, split, head_count - split, width
    )
    base, coarse = blend(
        gate_coarse,
        gate_fine,
        [half, third],
        [near_a, near_b],
        [pooled_a, pooled_b],
        5 if split % 5 == 0 else 1,
        width,
    )
    return patch(info, fetched, pairs, sums, coarse, base, head_count)


def solution(mesh):
    return jax.shard_map(
        per_device,
        mesh=mesh,
        in_specs=(
            P(("groups", "tm"), None),
            P(("groups", "tm"), None),
            P(("groups", "tm"), None),
            P(("groups", "tm"), None, None),
            P(),
            P(),
        ),
        out_specs=P(("groups", "tm"), None),
        check_vma=False,
    )
```

```python
import functools
import math

import jax
import jax.numpy as jnp
from jax import lax
from jax.experimental import pallas as pl
from jax.experimental.pallas import tpu as pltpu
from jax.sharding import PartitionSpec as P

CUBE = 64
CAP = 4
LOG2E = math.log2(math.e)
LANES = 128
PATCH_BATCH = 15
PRE_BATCH = 5
NEAR_STEP = 256
NEAR_WEIGHT = 20
GATHER_WEIGHT = 10**12
GATHER_BATCH = 8
MB = 1024 * 1024
SMALL = 6 * MB
LARGE = 56 * MB
F32 = jnp.float32
BF16 = jnp.bfloat16
I32 = jnp.int32


def vmem():
    return pl.BlockSpec(memory_space=pltpu.VMEM)


def smem():
    return pl.BlockSpec(memory_space=pltpu.SMEM)


def anywhere():
    return pl.BlockSpec(memory_space=pl.ANY)


def dot_t(a, b):
    return lax.dot_general(a, b, (((1,), (1,)), ((), ())), preferred_element_type=F32)


def dot_n(a, b):
    return lax.dot_general(a, b, (((1,), (0,)), ((), ())), preferred_element_type=F32)


def row_bits(head_count):
    return (head_count - 1).bit_length()


def plan_kernel(lists_hbm, codes_ref, slots_ref, kept_ref, lists_ref, sem):
    lists_load = pltpu.make_async_copy(lists_hbm, lists_ref, sem)
    lists_load.start()
    me = lax.axis_index("tm")
    cube_count, list_len, head_count = lists_ref.shape
    device_count = codes_ref.shape[0]
    cube_bits = cube_count.bit_length() - 1
    shift = row_bits(head_count)
    grid = (device_count, cube_count, head_count)
    flat = (device_count * cube_count, head_count)
    owner = lax.broadcasted_iota(I32, grid, 0)
    head = lax.broadcasted_iota(I32, grid, 2)
    square = (head_count, head_count)
    before = lax.broadcasted_iota(I32, square, 0) < lax.broadcasted_iota(I32, square, 1)
    before = jnp.where(before, 1.0, 0.0).astype(BF16)
    ones = jnp.ones(square, BF16)
    block = (flat[0], flat[0])
    high = lax.broadcasted_iota(I32, block, 0)
    low = lax.broadcasted_iota(I32, block, 1)
    same = lax.shift_right_logical(high, cube_bits) == lax.shift_right_logical(low, cube_bits)
    earlier = jnp.where(same & (low < high), 1.0, 0.0).astype(BF16)
    lane = lax.broadcasted_iota(I32, (head_count, LANES), 1)
    at_slots = [jnp.where(lane == slot, 1.0, 0.0).astype(BF16) for slot in range(CAP)]
    lists_load.wait()
    lists = lists_ref[...]
    far = lax.shift_right_arithmetic(lists, cube_bits) != me
    local = lists & (cube_count - 1)
    far_value = jnp.max(jnp.where(far, lists, -1), axis=1)
    value = jnp.broadcast_to(far_value[None], grid)
    hit = jnp.where(lax.shift_right_arithmetic(value, cube_bits) == owner, 1.0, 0.0)
    hit = hit.astype(F32).reshape(flat)
    hit_b = hit.astype(BF16)
    rank = dot_n(hit_b, before)
    total = dot_n(hit_b, ones)
    rank = rank + dot_n(earlier, total.astype(BF16))
    bits = jnp.where(far, 0, lax.shift_left(jnp.ones_like(local), local))
    kept_ref[...] = jnp.sum(bits, axis=1)
    code = lax.shift_left(value & (cube_count - 1), shift) | head
    code = (code + 1).astype(F32).reshape(flat) * hit
    chosen = [jnp.where(rank == float(slot), code, 0.0).astype(BF16) for slot in range(CAP)]
    codes = sum(dot_n(chosen[slot], at_slots[slot]) for slot in range(CAP))
    codes = jnp.sum(codes.reshape(device_count, cube_count, LANES), axis=1)
    codes_ref[...] = codes.astype(I32)
    slot_of = owner.astype(F32) * CAP + rank.reshape(grid) + 1.0
    slots_ref[...] = jnp.sum(slot_of * hit.reshape(grid), axis=0).astype(I32)


def plan(block_lists, device_count):
    lists = jnp.transpose(block_lists, (0, 2, 1))
    rows = jax.ShapeDtypeStruct(block_lists.shape[:2], I32)
    return pl.pallas_call(
        plan_kernel,
        out_shape=(jax.ShapeDtypeStruct((device_count, LANES), I32), rows, rows),
        in_specs=[anywhere()],
        out_specs=(vmem(),) * 3,
        scratch_shapes=[pltpu.VMEM(lists.shape, I32), pltpu.SemaphoreType.DMA],
        name="plan",
        compiler_params=pltpu.CompilerParams(vmem_limit_bytes=LARGE),
        cost_estimate=pl.CostEstimate(flops=1000000, bytes_accessed=64 * 1024, transcendentals=0),
    )(lists)


def pool_kernel(k_hbm, v_hbm, after_ref, pooled_ref, k_ref, v_ref, sums_ref, sems):
    cubes = pooled_ref.shape[1]
    loads = {}
    for cube in range(cubes):
        where = pl.ds(cube * CUBE, CUBE)
        for i, (source, target) in enumerate(((k_hbm, k_ref), (v_hbm, v_ref))):
            load = pltpu.make_async_copy(source.at[where], target.at[where], sems.at[i, cube])
            load.start()
            loads[i, cube] = load
    for cube in range(cubes):
        for i, target in enumerate((k_ref, v_ref)):
            loads[i, cube].wait()
            tokens = target[cube * CUBE : (cube + 1) * CUBE, :].astype(F32)
            sums_ref[i, cube : cube + 1, :] = jnp.sum(tokens, axis=0, keepdims=True)
    for i in range(2):
        pooled_ref[i] = (sums_ref[i] * (1.0 / CUBE)).astype(BF16)


def pool(keys, values, after):
    tokens, columns = keys.shape
    cubes = tokens // CUBE
    return pl.pallas_call(
        pool_kernel,
        out_shape=jax.ShapeDtypeStruct((2, cubes, columns), BF16),
        in_specs=[anywhere()] * 3,
        out_specs=vmem(),
        scratch_shapes=[
            pltpu.VMEM((tokens, columns), BF16),
            pltpu.VMEM((tokens, columns), BF16),
            pltpu.VMEM((2, cubes, columns), F32),
            pltpu.SemaphoreType.DMA((2, cubes)),
        ],
        name="pool",
        compiler_params=pltpu.CompilerParams(vmem_limit_bytes=LARGE),
        cost_estimate=pl.CostEstimate(
            flops=2 * keys.size, bytes_accessed=4 * keys.size, transcendentals=0
        ),
    )(keys, values, after)


def gather_kernel(
    shift,
    codes_hbm,
    k_hbm,
    v_hbm,
    after_ref,
    tiles_ref,
    done_ref,
    work_ref,
    codes_ref,
    slots_ref,
    load_sems,
    store_sem,
):
    slot_count, _, rows, width = tiles_ref.shape
    codes_load = pltpu.make_async_copy(codes_hbm, codes_ref, store_sem)
    codes_load.start()
    codes_load.wait()

    def scan(peer, found):
        for rank in range(CAP):
            slot = peer * CAP + rank
            code = codes_ref[peer, rank] - 1
            slots_ref[found] = slot

            @pl.when(code >= 0)
            def _():
                cube = lax.shift_right_logical(code, shift)
                head = code & ((1 << shift) - 1)
                where = (
                    pl.ds(pl.multiple_of(cube * rows, rows), rows),
                    pl.ds(pl.multiple_of(head * width, width), width),
                )
                sem = load_sems.at[found // GATHER_BATCH]
                pltpu.make_async_copy(k_hbm.at[where], work_ref.at[slot, 0], sem).start()
                pltpu.make_async_copy(v_hbm.at[where], work_ref.at[slot, 1], sem).start()

            found = found + (code >= 0).astype(I32)
        return found

    found = lax.fori_loop(0, slot_count // CAP, scan, jnp.int32(0))
    done_ref[...] = jnp.zeros_like(done_ref)

    def store_of(i):
        slot = slots_ref[i]
        return pltpu.make_async_copy(work_ref.at[slot], tiles_ref.at[slot], store_sem)

    @pl.loop(0, pl.cdiv(found, GATHER_BATCH))
    def _(batch):
        first = batch * GATHER_BATCH
        last = jnp.minimum(first + GATHER_BATCH, found)

        @pl.loop(first, last)
        def _(i):
            both = work_ref.at[slots_ref[i]]
            pltpu.make_async_copy(both, both, load_sems.at[batch]).wait()

        @pl.loop(first, last)
        def _(i):
            store_of(i).start()

    @pl.loop(0, found)
    def _(i):
        store_of(i).wait()


def gather_tiles(codes, keys, values, after, head_count):
    tokens, columns = keys.shape
    slot_count = codes.shape[0] * CAP
    shape = (slot_count, 2, CUBE, columns // head_count)
    return pl.pallas_call(
        functools.partial(gather_kernel, row_bits(head_count)),
        out_shape=(
            jax.ShapeDtypeStruct(shape, BF16),
            jax.ShapeDtypeStruct((8, LANES), F32),
        ),
        in_specs=[anywhere()] * 4,
        out_specs=(anywhere(), vmem()),
        scratch_shapes=[
            pltpu.VMEM(shape, BF16),
            pltpu.SMEM(codes.shape, I32),
            pltpu.SMEM((slot_count + 1,), I32),
            pltpu.SemaphoreType.DMA((pl.cdiv(slot_count, GATHER_BATCH),)),
            pltpu.SemaphoreType.DMA,
        ],
        name="gather_tiles",
        compiler_params=pltpu.CompilerParams(vmem_limit_bytes=LARGE),
        cost_estimate=pl.CostEstimate(
            flops=GATHER_WEIGHT, bytes_accessed=4 * math.prod(shape), transcendentals=0
        ),
    )(codes, keys, values, after)


def join_kernel(piece_count, *refs):
    out_ref = refs[-1]
    start = 0
    for piece in refs[:piece_count]:
        out_ref[start : start + piece.shape[0]] = piece[...]
        start += piece.shape[0]


def join(pieces, after=()):
    shape = (sum(piece.shape[0] for piece in pieces),) + pieces[0].shape[1:]
    return pl.pallas_call(
        functools.partial(join_kernel, len(pieces)),
        out_shape=jax.ShapeDtypeStruct(shape, BF16),
        in_specs=[vmem()] * len(pieces) + [anywhere()] * len(after),
        out_specs=vmem(),
        name="join",
        compiler_params=pltpu.CompilerParams(vmem_limit_bytes=SMALL),
        cost_estimate=pl.CostEstimate(
            flops=0, bytes_accessed=4 * math.prod(shape), transcendentals=0
        ),
    )(*pieces, *after)


def near_kernel(scale, q_ref, k_ref, v_ref, after_ref, out_ref, pooled_ref):
    tokens, width = q_ref.shape
    cubes = pooled_ref.shape[0]
    sums = jnp.sum(q_ref[...].astype(F32).reshape(cubes, CUBE, width), axis=1)
    pooled_ref[...] = (sums * (1.0 / CUBE)).astype(BF16)
    keys = k_ref[...]
    values = jnp.concatenate([v_ref[...], jnp.ones(v_ref.shape, BF16)], axis=1)
    step = NEAR_STEP
    starts = range(0, tokens, step)
    scores = dot_t(q_ref[0:step, :], keys)
    for start in starts:
        following = start + step
        if following < tokens:
            next_scores = dot_t(q_ref[following : following + step, :], keys)
        largest = jnp.max(scores, axis=1, keepdims=True)
        raised = jnp.exp2((scores - largest) * scale)
        mixed = dot_n(raised.astype(BF16), values)
        out_ref[start : start + step, :] = mixed[:, :width] / mixed[:, width:]
        if following < tokens:
            scores = next_scores


def near_attention(queries, keys, values, after, first, heads, width):
    tokens = queries.shape[0]
    block = pl.BlockSpec((tokens, width), lambda i: (0, first + i))
    return pl.pallas_call(
        functools.partial(near_kernel, width**-0.5 * LOG2E),
        out_shape=(
            jax.ShapeDtypeStruct((tokens, heads * width), F32),
            jax.ShapeDtypeStruct((tokens // CUBE, heads * width), BF16),
        ),
        grid=(heads,),
        in_specs=[block] * 3 + [anywhere()],
        out_specs=(
            pl.BlockSpec((tokens, width), lambda i: (0, i)),
            pl.BlockSpec((tokens // CUBE, width), lambda i: (0, i)),
        ),
        name="near_attention",
        compiler_params=pltpu.CompilerParams(vmem_limit_bytes=SMALL),
        cost_estimate=pl.CostEstimate(
            flops=NEAR_WEIGHT * 4 * tokens * tokens * heads * width,
            bytes_accessed=10 * tokens * heads * width,
            transcendentals=tokens * tokens * heads,
        ),
    )(queries, keys, values, after)


class Part:
    def __init__(self, ref, start):
        self.ref, self.start = ref, start

    def __getitem__(self, i):
        return self.ref[self.start + i]

    def __setitem__(self, i, value):
        self.ref[self.start + i] = value


def list_parts(info_ref, dense):
    return Part(info_ref, 0), Part(info_ref, dense), 2 * dense


def pre_kernel(
    scale,
    shift,
    slot_of_ref,
    kept_ref,
    q_ref,
    k_ref,
    v_ref,
    after_ref,
    info_ref,
    pairs_ref,
    sums_ref,
    sets_ref,
):
    cube_count, head_count = slot_of_ref.shape
    dense, _, width = sums_ref.shape
    tokens = q_ref.shape[0]
    slots_ref, rows_ref, count_at = list_parts(info_ref, dense)
    slots_ref[0] = 1
    rows_ref[0] = 0
    sets_ref[0] = 1

    def scan(cube, found):
        for head in range(head_count):
            slot = slot_of_ref[cube, head]
            slots_ref[found] = slot
            rows_ref[found] = lax.shift_left(cube, shift) | head
            sets_ref[found] = kept_ref[cube, head]
            found = found + (slot > 0).astype(I32)
        return found

    found = lax.fori_loop(0, cube_count, scan, jnp.int32(0))
    info_ref[count_at] = found
    last = jnp.maximum(found - 1, 0)
    for more in range(PATCH_BATCH):
        slots_ref[found + more] = slots_ref[last]
        rows_ref[found + more] = rows_ref[last]
        sets_ref[found + more] = sets_ref[last]
    cube_of = lax.broadcasted_iota(I32, (1, tokens), 1) // CUBE

    @pl.loop(0, pl.cdiv(found, PATCH_BATCH) * (PATCH_BATCH // PRE_BATCH))
    def _(step):
        first = step * PRE_BATCH
        parts = range(PRE_BATCH)
        codes = [rows_ref[first + part] for part in parts]
        cubes = [lax.shift_right_logical(code, shift) for code in codes]
        heads = [code & ((1 << shift) - 1) for code in codes]
        columns = [pl.ds(pl.multiple_of(head * width, width), width) for head in heads]
        queries = [
            q_ref[pl.ds(pl.multiple_of(cubes[part] * CUBE, CUBE), CUBE), columns[part]]
            for part in parts
        ]
        scores = [dot_t(queries[part], k_ref[:, columns[part]]) for part in parts]
        for part in parts:
            kept = (lax.shift_right_logical(sets_ref[first + part], cube_of) & 1) > 0
            scores[part] = jnp.where(kept, scores[part], -3e38)
        largest = [jnp.max(score, axis=1, keepdims=True) for score in scores]
        raised = [
            jnp.exp2((scores[part] - largest[part]) * scale).astype(BF16) for part in parts
        ]
        ones = jnp.ones((tokens, width), BF16)
        values = [jnp.concatenate([v_ref[:, columns[part]], ones], axis=1) for part in parts]
        mixed = [dot_n(raised[part], values[part]) for part in parts]
        for part in parts:
            pairs_ref[first + part, 0] = queries[part]
            total = mixed[part][:, width:]
            pairs_ref[first + part, 1] = (mixed[part][:, :width] / total).astype(BF16)
            sums_ref[first + part] = largest[part] * scale + jnp.log2(total)


def far_rows(slot_of, kept, queries, keys, values, after, slot_count):
    tokens, columns = queries.shape
    head_count = slot_of.shape[1]
    width = columns // head_count
    dense = (slot_count // PATCH_BATCH + 2) * PATCH_BATCH
    return pl.pallas_call(
        functools.partial(pre_kernel, width**-0.5 * LOG2E, row_bits(head_count)),
        out_shape=(
            jax.ShapeDtypeStruct((2 * dense + 1,), I32),
            jax.ShapeDtypeStruct((dense, 2, CUBE, width), BF16),
            jax.ShapeDtypeStruct((dense, CUBE, width), F32),
        ),
        in_specs=[smem(), smem(), vmem(), vmem(), vmem(), anywhere()],
        out_specs=(smem(), vmem(), vmem()),
        scratch_shapes=[pltpu.SMEM((dense,), I32)],
        name="far_rows",
        compiler_params=pltpu.CompilerParams(vmem_limit_bytes=SMALL),
        cost_estimate=pl.CostEstimate(
            flops=4 * slot_count * CUBE * tokens * width,
            bytes_accessed=6 * tokens * columns,
            transcendentals=slot_count * CUBE * tokens,
        ),
    )(slot_of, kept, queries, keys, values, after)


def blend_kernel(scale, heads, pieces, parts, gc_ref, gf_ref, *refs):
    key_refs, value_refs = refs[:pieces], refs[pieces : 2 * pieces]
    near_refs = refs[2 * pieces : 2 * pieces + parts]
    query_refs = refs[2 * pieces + parts : 2 * pieces + 2 * parts]
    out_ref, coarse_ref = refs[2 * pieces + 2 * parts :]
    cube_count, columns = coarse_ref.shape[0] // 2, coarse_ref.shape[1]
    width = columns // heads
    first = pl.program_id(0) * heads
    places = [slice(part * width, (part + 1) * width) for part in range(heads)]

    def gathered(piece_refs, here):
        flat = [ref[:, 0, :, here].reshape(-1, width) for ref in piece_refs]
        return jnp.concatenate(flat, axis=0)

    def put(near_ref, query_ref):
        keys = [gathered(key_refs, here) for here in places]
        values = [gathered(value_refs, here) for here in places]
        scores = [dot_t(query_ref[:, here], key) for here, key in zip(places, keys)]
        scores = jnp.concatenate(scores, axis=0) * scale
        largest = jnp.max(scores, axis=1, keepdims=True)
        raised = jnp.exp(scores - largest)
        weights = raised / jnp.sum(raised, axis=1, keepdims=True)
        coarse = []
        for part in range(heads):
            mine = weights[part * cube_count : (part + 1) * cube_count].astype(BF16)
            coarse.append(gc_ref[first + part] * dot_n(mine, values[part]))
        for part, here in enumerate(places):
            coarse_ref[:cube_count, here] = coarse[part]
            gate = jnp.full((cube_count, width), gf_ref[first + part], F32)
            coarse_ref[cube_count:, here] = gate
            near = near_ref[:, here].reshape(cube_count, CUBE, width)
            blended = coarse[part][:, None, :] + gf_ref[first + part] * near
            out_ref[:, here] = blended.reshape(cube_count * CUBE, width).astype(BF16)

    share = pl.num_programs(0) // parts
    for part in range(parts):
        chosen = functools.partial(put, near_refs[part], query_refs[part])
        pl.when(pl.program_id(0) // share == part)(chosen)


def blend(gate_coarse, gate_fine, pieces, nears, pooled_queries, heads, width):
    tokens, part_columns = nears[0].shape
    cube_count = tokens // CUBE
    columns = part_columns * len(nears)
    step = heads * width
    share = part_columns // step

    def piece_spec(piece, which):
        shape = (piece.shape[0], 1, cube_count, step)
        return pl.BlockSpec(shape, lambda i: (0, which, 0, i))

    def part_spec(rows, part):
        return pl.BlockSpec(
            (rows, step), lambda i: (0, jnp.clip(i - part * share, 0, share - 1))
        )

    parts = range(len(nears))
    return pl.pallas_call(
        functools.partial(blend_kernel, width**-0.5, heads, len(pieces), len(nears)),
        out_shape=(
            jax.ShapeDtypeStruct((tokens, columns), BF16),
            jax.ShapeDtypeStruct((2 * cube_count, columns), F32),
        ),
        grid=(columns // step,),
        in_specs=[smem(), smem()]
        + [piece_spec(piece, 0) for piece in pieces]
        + [piece_spec(piece, 1) for piece in pieces]
        + [part_spec(tokens, part) for part in parts]
        + [part_spec(cube_count, part) for part in parts],
        out_specs=(
            pl.BlockSpec((tokens, step), lambda i: (0, i)),
            pl.BlockSpec((2 * cube_count, step), lambda i: (0, i)),
        ),
        name="blend",
        compiler_params=pltpu.CompilerParams(vmem_limit_bytes=16 * MB),
        cost_estimate=pl.CostEstimate(
            flops=2 * tokens * columns, bytes_accessed=6 * tokens * columns, transcendentals=0
        ),
    )(gate_coarse, gate_fine, *pieces, *pieces, *nears, *pooled_queries)


def patch_kernel(
    scale,
    shift,
    info_ref,
    tiles_hbm,
    pairs_hbm,
    sums_hbm,
    coarse_hbm,
    base_ref,
    out_ref,
    tiles_ref,
    pairs_ref,
    sums_ref,
    coarse_ref,
    ready_ref,
    load_sems,
    coarse_sem,
    store_sem,
):
    dense, _, width = sums_ref.shape
    cube_count = coarse_ref.shape[0] // 2
    slots_ref, rows_ref, count_at = list_parts(info_ref, dense)
    count = info_ref[count_at]
    steps = pl.cdiv(count, PATCH_BATCH)
    coarse_load = pltpu.make_async_copy(coarse_hbm, coarse_ref, coarse_sem)

    def batch_load(step, which):
        source, target = ((pairs_hbm, pairs_ref), (sums_hbm, sums_ref))[which]
        where = pl.ds(step * PATCH_BATCH, PATCH_BATCH)
        return pltpu.make_async_copy(source.at[where], target.at[where], load_sems.at[which, step])

    def store(i):
        row = rows_ref[i]
        cube = lax.shift_right_logical(row, shift)
        head = row & ((1 << shift) - 1)
        where = (
            pl.ds(pl.multiple_of(cube * CUBE, CUBE), CUBE),
            pl.ds(pl.multiple_of(head * width, width), width),
        )
        return pltpu.make_async_copy(ready_ref.at[i], out_ref.at[where], store_sem)

    @pl.loop(0, steps)
    def _(step):
        for which in range(2):
            batch_load(step, which).start()
        for part in range(PATCH_BATCH):
            i = step * PATCH_BATCH + part
            tile = tiles_hbm.at[slots_ref[i] - 1]
            pltpu.make_async_copy(tile, tiles_ref.at[i], load_sems.at[2, step]).start()

        @pl.when(step == 0)
        def _():
            coarse_load.start()

    @pl.loop(0, steps)
    def _(step):
        @pl.when(step == 0)
        def _():
            coarse_load.wait()

        first = step * PATCH_BATCH
        parts = range(PATCH_BATCH)
        for which in range(2):
            batch_load(step, which).wait()
        tiles = tiles_ref.at[pl.ds(first, PATCH_BATCH)]
        pltpu.make_async_copy(tiles, tiles, load_sems.at[2, step]).wait()
        codes = [rows_ref[first + part] for part in parts]
        cubes = [lax.shift_right_logical(code, shift) for code in codes]
        heads = [code & ((1 << shift) - 1) for code in codes]
        columns = [pl.ds(pl.multiple_of(head * width, width), width) for head in heads]
        scores = [dot_t(pairs_ref[first + part, 0], tiles_ref[first + part, 0]) for part in parts]
        scores = [score * scale for score in scores]
        tops = [jnp.max(score, axis=1, keepdims=True) for score in scores]
        sums = [sums_ref[first + part] for part in parts]
        largest = [jnp.maximum(sums[part], tops[part]) for part in parts]
        raised = [
            jnp.exp2(scores[part] - largest[part][:, :CUBE]).astype(BF16) for part in parts
        ]
        ones = jnp.ones((CUBE, width), BF16)
        values = [jnp.concatenate([tiles_ref[first + part, 1], ones], axis=1) for part in parts]
        mixed = [dot_n(raised[part], values[part]) for part in parts]
        for part in parts:
            coarse = coarse_ref[:cube_count, columns[part]]
            gate = coarse_ref[cube_count : cube_count + 1, columns[part]]
            this_cube = lax.broadcasted_iota(I32, coarse.shape, 0) == cubes[part]
            coarse = jnp.sum(jnp.where(this_cube, coarse, 0.0), axis=0, keepdims=True)
            kept = jnp.exp2(sums[part] - largest[part])
            total = kept + mixed[part][:, width:]
            fine = pairs_ref[first + part, 1].astype(F32) * kept + mixed[part][:, :width]
            blended = coarse + gate * (fine / total)
            ready_ref[first + part] = blended.astype(BF16)
        for part in parts:
            pl.when(first + part < count)(store(first + part).start)

    @pl.loop(0, count)
    def _(i):
        store(i).wait()


def patch(info, tiles, pairs, sums, coarse, base, head_count):
    dense, _, width = sums.shape
    return pl.pallas_call(
        functools.partial(patch_kernel, width**-0.5 * LOG2E, row_bits(head_count)),
        out_shape=jax.ShapeDtypeStruct(base.shape, BF16),
        in_specs=[smem()] + [anywhere()] * 5,
        out_specs=anywhere(),
        scratch_shapes=[
            pltpu.VMEM((dense,) + tiles.shape[1:], BF16),
            pltpu.VMEM(pairs.shape, BF16),
            pltpu.VMEM(sums.shape, F32),
            pltpu.VMEM(coarse.shape, F32),
            pltpu.VMEM((dense, CUBE, width), BF16),
            pltpu.SemaphoreType.DMA((3, dense // PATCH_BATCH)),
            pltpu.SemaphoreType.DMA,
            pltpu.SemaphoreType.DMA,
        ],
        input_output_aliases={5: 0},
        name="patch",
        compiler_params=pltpu.CompilerParams(vmem_limit_bytes=LARGE),
        cost_estimate=pl.CostEstimate(
            flops=4 * dense * CUBE * CUBE * width,
            bytes_accessed=16 * dense * CUBE * width,
            transcendentals=dense * CUBE * CUBE,
        ),
    )(info, tiles, pairs, sums, coarse, base)


def per_device(queries, keys, values, block_lists, gate_coarse, gate_fine):
    head_count = gate_coarse.shape[0]
    width = queries.shape[1] // head_count
    cube_count = block_lists.shape[0]
    device_count = lax.axis_size("tm")
    codes, slot_of, kept = plan(block_lists, device_count)
    wanted = lax.all_to_all(codes, "tm", split_axis=0, concat_axis=0, tiled=True)
    pooled_pairs = pool(keys, values, codes)

    def exchange(array, mask):
        return lax.ppermute(array, "tm", [(i, i ^ mask) for i in range(device_count)])

    own = pooled_pairs[None]
    across = exchange(own, device_count // 2)
    masks = range(4, device_count // 2, 4)
    received = [exchange(own, mask) for mask in masks]
    tiles, after = gather_tiles(wanted, keys, values, pooled_pairs, head_count)
    tiles, across = lax.optimization_barrier((tiles, across))
    received += [exchange(across, mask) for mask in masks]
    fetched = lax.all_to_all(tiles, "tm", split_axis=0, concat_axis=0, tiled=True)
    quarter = join([own, across] + received, after=(after,))
    second = exchange(quarter, 2)
    info, pairs, sums = far_rows(slot_of, kept, queries, keys, values, quarter, device_count * CAP)
    split = head_count // 2
    near_a, pooled_a = near_attention(queries, keys, values, quarter, 0, split, width)
    half = join([quarter, second], after=(near_a, sums))
    third = exchange(half, 1)
    near_b, pooled_b = near_attention(
        queries, keys, values, half, split, head_count - split, width
    )
    base, coarse = blend(
        gate_coarse,
        gate_fine,
        [half, third],
        [near_a, near_b],
        [pooled_a, pooled_b],
        5 if split % 5 == 0 else 1,
        width,
    )
    return patch(info, fetched, pairs, sums, coarse, base, head_count)


def solution(mesh):
    return jax.shard_map(
        per_device,
        mesh=mesh,
        in_specs=(
            P(("groups", "tm"), None),
            P(("groups", "tm"), None),
            P(("groups", "tm"), None),
            P(("groups", "tm"), None, None),
            P(),
            P(),
        ),
        out_specs=P(("groups", "tm"), None),
        check_vma=False,
    )
```

```python
import functools
import math

import jax
import jax.numpy as jnp
from jax import lax
from jax.experimental import pallas as pl
from jax.experimental.pallas import tpu as pltpu
from jax.sharding import PartitionSpec as P

CUBE = 64
CAP = 4
LOG2E = math.log2(math.e)
LANES = 128
PATCH_BATCH = 15
PRE_BATCH = 5
NEAR_STEP = 256
NEAR_WEIGHT = 20
GATHER_WEIGHT = 10**12
GATHER_BATCH = 8
MB = 1024 * 1024
SMALL = 6 * MB
LARGE = 56 * MB
F32 = jnp.float32
BF16 = jnp.bfloat16
I32 = jnp.int32


def vmem():
    return pl.BlockSpec(memory_space=pltpu.VMEM)


def smem():
    return pl.BlockSpec(memory_space=pltpu.SMEM)


def anywhere():
    return pl.BlockSpec(memory_space=pl.ANY)


def dot_t(a, b):
    return lax.dot_general(a, b, (((1,), (1,)), ((), ())), preferred_element_type=F32)


def dot_n(a, b):
    return lax.dot_general(a, b, (((1,), (0,)), ((), ())), preferred_element_type=F32)


def row_bits(head_count):
    return (head_count - 1).bit_length()


def plan_kernel(lists_hbm, codes_ref, slots_ref, kept_ref, lists_ref, sem):
    lists_load = pltpu.make_async_copy(lists_hbm, lists_ref, sem)
    lists_load.start()
    me = lax.axis_index("tm")
    cube_count, list_len, head_count = lists_ref.shape
    device_count = codes_ref.shape[0]
    cube_bits = cube_count.bit_length() - 1
    shift = row_bits(head_count)
    grid = (device_count, cube_count, head_count)
    flat = (device_count * cube_count, head_count)
    owner = lax.broadcasted_iota(I32, grid, 0)
    head = lax.broadcasted_iota(I32, grid, 2)
    square = (head_count, head_count)
    before = lax.broadcasted_iota(I32, square, 0) < lax.broadcasted_iota(I32, square, 1)
    before = jnp.where(before, 1.0, 0.0).astype(BF16)
    ones = jnp.ones(square, BF16)
    block = (flat[0], flat[0])
    high = lax.broadcasted_iota(I32, block, 0)
    low = lax.broadcasted_iota(I32, block, 1)
    same = lax.shift_right_logical(high, cube_bits) == lax.shift_right_logical(low, cube_bits)
    earlier = jnp.where(same & (low < high), 1.0, 0.0).astype(BF16)
    lane = lax.broadcasted_iota(I32, (head_count, LANES), 1)
    at_slots = [jnp.where(lane == slot, 1.0, 0.0).astype(BF16) for slot in range(CAP)]
    lists_load.wait()
    lists = lists_ref[...]
    far = lax.shift_right_arithmetic(lists, cube_bits) != me
    local = lists & (cube_count - 1)
    far_value = jnp.max(jnp.where(far, lists, -1), axis=1)
    value = jnp.broadcast_to(far_value[None], grid)
    hit = jnp.where(lax.shift_right_arithmetic(value, cube_bits) == owner, 1.0, 0.0)
    hit = hit.astype(F32).reshape(flat)
    hit_b = hit.astype(BF16)
    rank = dot_n(hit_b, before)
    total = dot_n(hit_b, ones)
    rank = rank + dot_n(earlier, total.astype(BF16))
    bits = jnp.where(far, 0, lax.shift_left(jnp.ones_like(local), local))
    kept_ref[...] = jnp.sum(bits, axis=1)
    code = lax.shift_left(value & (cube_count - 1), shift) | head
    code = (code + 1).astype(F32).reshape(flat) * hit
    chosen = [jnp.where(rank == float(slot), code, 0.0).astype(BF16) for slot in range(CAP)]
    codes = sum(dot_n(chosen[slot], at_slots[slot]) for slot in range(CAP))
    codes = jnp.sum(codes.reshape(device_count, cube_count, LANES), axis=1)
    codes_ref[...] = codes.astype(I32)
    slot_of = owner.astype(F32) * CAP + rank.reshape(grid) + 1.0
    slots_ref[...] = jnp.sum(slot_of * hit.reshape(grid), axis=0).astype(I32)


def plan(block_lists, device_count):
    lists = jnp.transpose(block_lists, (0, 2, 1))
    rows = jax.ShapeDtypeStruct(block_lists.shape[:2], I32)
    return pl.pallas_call(
        plan_kernel,
        out_shape=(jax.ShapeDtypeStruct((device_count, LANES), I32), rows, rows),
        in_specs=[anywhere()],
        out_specs=(vmem(),) * 3,
        scratch_shapes=[pltpu.VMEM(lists.shape, I32), pltpu.SemaphoreType.DMA],
        name="plan",
        compiler_params=pltpu.CompilerParams(vmem_limit_bytes=LARGE),
        cost_estimate=pl.CostEstimate(flops=1000000, bytes_accessed=64 * 1024, transcendentals=0),
    )(lists)


def pool_kernel(k_hbm, v_hbm, after_ref, pooled_ref, k_ref, v_ref, sums_ref, sems):
    cubes = pooled_ref.shape[1]
    loads = {}
    for cube in range(cubes):
        where = pl.ds(cube * CUBE, CUBE)
        for i, (source, target) in enumerate(((k_hbm, k_ref), (v_hbm, v_ref))):
            load = pltpu.make_async_copy(source.at[where], target.at[where], sems.at[i, cube])
            load.start()
            loads[i, cube] = load
    for cube in range(cubes):
        for i, target in enumerate((k_ref, v_ref)):
            loads[i, cube].wait()
            tokens = target[cube * CUBE : (cube + 1) * CUBE, :].astype(F32)
            sums_ref[i, cube : cube + 1, :] = jnp.sum(tokens, axis=0, keepdims=True)
    for i in range(2):
        pooled_ref[i] = (sums_ref[i] * (1.0 / CUBE)).astype(BF16)


def pool(keys, values, after):
    tokens, columns = keys.shape
    cubes = tokens // CUBE
    return pl.pallas_call(
        pool_kernel,
        out_shape=jax.ShapeDtypeStruct((2, cubes, columns), BF16),
        in_specs=[anywhere()] * 3,
        out_specs=vmem(),
        scratch_shapes=[
            pltpu.VMEM((tokens, columns), BF16),
            pltpu.VMEM((tokens, columns), BF16),
            pltpu.VMEM((2, cubes, columns), F32),
            pltpu.SemaphoreType.DMA((2, cubes)),
        ],
        name="pool",
        compiler_params=pltpu.CompilerParams(vmem_limit_bytes=LARGE),
        cost_estimate=pl.CostEstimate(
            flops=2 * keys.size, bytes_accessed=4 * keys.size, transcendentals=0
        ),
    )(keys, values, after)


def gather_kernel(
    shift,
    codes_hbm,
    k_hbm,
    v_hbm,
    after_ref,
    tiles_ref,
    done_ref,
    work_ref,
    codes_ref,
    slots_ref,
    load_sems,
    store_sem,
):
    slot_count, _, rows, width = tiles_ref.shape
    codes_load = pltpu.make_async_copy(codes_hbm, codes_ref, store_sem)
    codes_load.start()
    codes_load.wait()

    def scan(peer, found):
        for rank in range(CAP):
            slot = peer * CAP + rank
            code = codes_ref[peer, rank] - 1
            slots_ref[found] = slot

            @pl.when(code >= 0)
            def _():
                cube = lax.shift_right_logical(code, shift)
                head = code & ((1 << shift) - 1)
                where = (
                    pl.ds(pl.multiple_of(cube * rows, rows), rows),
                    pl.ds(pl.multiple_of(head * width, width), width),
                )
                sem = load_sems.at[found // GATHER_BATCH]
                pltpu.make_async_copy(k_hbm.at[where], work_ref.at[slot, 0], sem).start()
                pltpu.make_async_copy(v_hbm.at[where], work_ref.at[slot, 1], sem).start()

            found = found + (code >= 0).astype(I32)
        return found

    found = lax.fori_loop(0, slot_count // CAP, scan, jnp.int32(0))
    done_ref[...] = jnp.zeros_like(done_ref)

    def store_of(i):
        slot = slots_ref[i]
        return pltpu.make_async_copy(work_ref.at[slot], tiles_ref.at[slot], store_sem)

    @pl.loop(0, pl.cdiv(found, GATHER_BATCH))
    def _(batch):
        first = batch * GATHER_BATCH
        last = jnp.minimum(first + GATHER_BATCH, found)

        @pl.loop(first, last)
        def _(i):
            both = work_ref.at[slots_ref[i]]
            pltpu.make_async_copy(both, both, load_sems.at[batch]).wait()

        @pl.loop(first, last)
        def _(i):
            store_of(i).start()

    @pl.loop(0, found)
    def _(i):
        store_of(i).wait()


def gather_tiles(codes, keys, values, after, head_count):
    tokens, columns = keys.shape
    slot_count = codes.shape[0] * CAP
    shape = (slot_count, 2, CUBE, columns // head_count)
    return pl.pallas_call(
        functools.partial(gather_kernel, row_bits(head_count)),
        out_shape=(
            jax.ShapeDtypeStruct(shape, BF16),
            jax.ShapeDtypeStruct((8, LANES), F32),
        ),
        in_specs=[anywhere()] * 4,
        out_specs=(anywhere(), vmem()),
        scratch_shapes=[
            pltpu.VMEM(shape, BF16),
            pltpu.SMEM(codes.shape, I32),
            pltpu.SMEM((slot_count + 1,), I32),
            pltpu.SemaphoreType.DMA((pl.cdiv(slot_count, GATHER_BATCH),)),
            pltpu.SemaphoreType.DMA,
        ],
        name="gather_tiles",
        compiler_params=pltpu.CompilerParams(vmem_limit_bytes=64 * MB),
        cost_estimate=pl.CostEstimate(
            flops=GATHER_WEIGHT, bytes_accessed=4 * math.prod(shape), transcendentals=0
        ),
    )(codes, keys, values, after)


def join_kernel(piece_count, *refs):
    out_ref = refs[-1]
    start = 0
    for piece in refs[:piece_count]:
        out_ref[start : start + piece.shape[0]] = piece[...]
        start += piece.shape[0]


def join(pieces, after=()):
    shape = (sum(piece.shape[0] for piece in pieces),) + pieces[0].shape[1:]
    return pl.pallas_call(
        functools.partial(join_kernel, len(pieces)),
        out_shape=jax.ShapeDtypeStruct(shape, BF16),
        in_specs=[vmem()] * len(pieces) + [anywhere()] * len(after),
        out_specs=vmem(),
        name="join",
        compiler_params=pltpu.CompilerParams(vmem_limit_bytes=SMALL),
        cost_estimate=pl.CostEstimate(
            flops=0, bytes_accessed=4 * math.prod(shape), transcendentals=0
        ),
    )(*pieces, *after)


def near_kernel(scale, q_ref, k_ref, v_ref, after_ref, out_ref, pooled_ref):
    tokens, width = q_ref.shape
    cubes = pooled_ref.shape[0]
    sums = jnp.sum(q_ref[...].astype(F32).reshape(cubes, CUBE, width), axis=1)
    pooled_ref[...] = (sums * (1.0 / CUBE)).astype(BF16)
    keys = k_ref[...]
    values = jnp.concatenate([v_ref[...], jnp.ones(v_ref.shape, BF16)], axis=1)
    step = NEAR_STEP
    starts = range(0, tokens, step)
    scores = dot_t(q_ref[0:step, :], keys)
    for start in starts:
        following = start + step
        if following < tokens:
            next_scores = dot_t(q_ref[following : following + step, :], keys)
        largest = jnp.max(scores, axis=1, keepdims=True)
        raised = jnp.exp2((scores - largest) * scale)
        mixed = dot_n(raised.astype(BF16), values)
        out_ref[start : start + step, :] = mixed[:, :width] / mixed[:, width:]
        if following < tokens:
            scores = next_scores


def near_attention(queries, keys, values, after, first, heads, width):
    tokens = queries.shape[0]
    block = pl.BlockSpec((tokens, width), lambda i: (0, first + i))
    return pl.pallas_call(
        functools.partial(near_kernel, width**-0.5 * LOG2E),
        out_shape=(
            jax.ShapeDtypeStruct((tokens, heads * width), F32),
            jax.ShapeDtypeStruct((tokens // CUBE, heads * width), BF16),
        ),
        grid=(heads,),
        in_specs=[block] * 3 + [anywhere()],
        out_specs=(
            pl.BlockSpec((tokens, width), lambda i: (0, i)),
            pl.BlockSpec((tokens // CUBE, width), lambda i: (0, i)),
        ),
        name="near_attention",
        compiler_params=pltpu.CompilerParams(vmem_limit_bytes=SMALL),
        cost_estimate=pl.CostEstimate(
            flops=NEAR_WEIGHT * 4 * tokens * tokens * heads * width,
            bytes_accessed=10 * tokens * heads * width,
            transcendentals=tokens * tokens * heads,
        ),
    )(queries, keys, values, after)


class Part:
    def __init__(self, ref, start):
        self.ref, self.start = ref, start

    def __getitem__(self, i):
        return self.ref[self.start + i]

    def __setitem__(self, i, value):
        self.ref[self.start + i] = value


def list_parts(info_ref, dense):
    return Part(info_ref, 0), Part(info_ref, dense), 2 * dense


def pre_kernel(
    scale,
    shift,
    slot_of_ref,
    kept_ref,
    q_ref,
    k_ref,
    v_ref,
    after_ref,
    info_ref,
    pairs_ref,
    sums_ref,
    sets_ref,
):
    cube_count, head_count = slot_of_ref.shape
    dense, _, width = sums_ref.shape
    tokens = q_ref.shape[0]
    slots_ref, rows_ref, count_at = list_parts(info_ref, dense)
    slots_ref[0] = 1
    rows_ref[0] = 0
    sets_ref[0] = 1

    def scan(cube, found):
        for head in range(head_count):
            slot = slot_of_ref[cube, head]
            slots_ref[found] = slot
            rows_ref[found] = lax.shift_left(cube, shift) | head
            sets_ref[found] = kept_ref[cube, head]
            found = found + (slot > 0).astype(I32)
        return found

    found = lax.fori_loop(0, cube_count, scan, jnp.int32(0))
    info_ref[count_at] = found
    last = jnp.maximum(found - 1, 0)
    for more in range(PATCH_BATCH):
        slots_ref[found + more] = slots_ref[last]
        rows_ref[found + more] = rows_ref[last]
        sets_ref[found + more] = sets_ref[last]
    cube_of = lax.broadcasted_iota(I32, (1, tokens), 1) // CUBE

    @pl.loop(0, pl.cdiv(found, PATCH_BATCH) * (PATCH_BATCH // PRE_BATCH))
    def _(step):
        first = step * PRE_BATCH
        parts = range(PRE_BATCH)
        codes = [rows_ref[first + part] for part in parts]
        cubes = [lax.shift_right_logical(code, shift) for code in codes]
        heads = [code & ((1 << shift) - 1) for code in codes]
        columns = [pl.ds(pl.multiple_of(head * width, width), width) for head in heads]
        queries = [
            q_ref[pl.ds(pl.multiple_of(cubes[part] * CUBE, CUBE), CUBE), columns[part]]
            for part in parts
        ]
        scores = [dot_t(queries[part], k_ref[:, columns[part]]) for part in parts]
        for part in parts:
            kept = (lax.shift_right_logical(sets_ref[first + part], cube_of) & 1) > 0
            scores[part] = jnp.where(kept, scores[part], -3e38)
        largest = [jnp.max(score, axis=1, keepdims=True) for score in scores]
        raised = [
            jnp.exp2((scores[part] - largest[part]) * scale).astype(BF16) for part in parts
        ]
        ones = jnp.ones((tokens, width), BF16)
        values = [jnp.concatenate([v_ref[:, columns[part]], ones], axis=1) for part in parts]
        mixed = [dot_n(raised[part], values[part]) for part in parts]
        for part in parts:
            pairs_ref[first + part, 0] = queries[part]
            total = mixed[part][:, width:]
            pairs_ref[first + part, 1] = (mixed[part][:, :width] / total).astype(BF16)
            sums_ref[first + part] = largest[part] * scale + jnp.log2(total)


def far_rows(slot_of, kept, queries, keys, values, after, slot_count):
    tokens, columns = queries.shape
    head_count = slot_of.shape[1]
    width = columns // head_count
    dense = (slot_count // PATCH_BATCH + 2) * PATCH_BATCH
    return pl.pallas_call(
        functools.partial(pre_kernel, width**-0.5 * LOG2E, row_bits(head_count)),
        out_shape=(
            jax.ShapeDtypeStruct((2 * dense + 1,), I32),
            jax.ShapeDtypeStruct((dense, 2, CUBE, width), BF16),
            jax.ShapeDtypeStruct((dense, CUBE, width), F32),
        ),
        in_specs=[smem(), smem(), vmem(), vmem(), vmem(), anywhere()],
        out_specs=(smem(), vmem(), vmem()),
        scratch_shapes=[pltpu.SMEM((dense,), I32)],
        name="far_rows",
        compiler_params=pltpu.CompilerParams(vmem_limit_bytes=SMALL),
        cost_estimate=pl.CostEstimate(
            flops=4 * slot_count * CUBE * tokens * width,
            bytes_accessed=6 * tokens * columns,
            transcendentals=slot_count * CUBE * tokens,
        ),
    )(slot_of, kept, queries, keys, values, after)


def blend_kernel(scale, heads, pieces, parts, gc_ref, gf_ref, *refs):
    key_refs, value_refs = refs[:pieces], refs[pieces : 2 * pieces]
    near_refs = refs[2 * pieces : 2 * pieces + parts]
    query_refs = refs[2 * pieces + parts : 2 * pieces + 2 * parts]
    out_ref, coarse_ref = refs[2 * pieces + 2 * parts :]
    cube_count, columns = coarse_ref.shape[0] // 2, coarse_ref.shape[1]
    width = columns // heads
    first = pl.program_id(0) * heads
    places = [slice(part * width, (part + 1) * width) for part in range(heads)]

    def gathered(piece_refs, here):
        flat = [ref[:, 0, :, here].reshape(-1, width) for ref in piece_refs]
        return jnp.concatenate(flat, axis=0)

    def put(near_ref, query_ref):
        keys = [gathered(key_refs, here) for here in places]
        values = [gathered(value_refs, here) for here in places]
        scores = [dot_t(query_ref[:, here], key) for here, key in zip(places, keys)]
        scores = jnp.concatenate(scores, axis=0) * scale
        largest = jnp.max(scores, axis=1, keepdims=True)
        raised = jnp.exp(scores - largest)
        weights = raised / jnp.sum(raised, axis=1, keepdims=True)
        coarse = []
        for part in range(heads):
            mine = weights[part * cube_count : (part + 1) * cube_count].astype(BF16)
            coarse.append(gc_ref[first + part] * dot_n(mine, values[part]))
        for part, here in enumerate(places):
            coarse_ref[:cube_count, here] = coarse[part]
            gate = jnp.full((cube_count, width), gf_ref[first + part], F32)
            coarse_ref[cube_count:, here] = gate
            near = near_ref[:, here].reshape(cube_count, CUBE, width)
            blended = coarse[part][:, None, :] + gf_ref[first + part] * near
            out_ref[:, here] = blended.reshape(cube_count * CUBE, width).astype(BF16)

    share = pl.num_programs(0) // parts
    for part in range(parts):
        chosen = functools.partial(put, near_refs[part], query_refs[part])
        pl.when(pl.program_id(0) // share == part)(chosen)


def blend(gate_coarse, gate_fine, pieces, nears, pooled_queries, heads, width):
    tokens, part_columns = nears[0].shape
    cube_count = tokens // CUBE
    columns = part_columns * len(nears)
    step = heads * width
    share = part_columns // step

    def piece_spec(piece, which):
        shape = (piece.shape[0], 1, cube_count, step)
        return pl.BlockSpec(shape, lambda i: (0, which, 0, i))

    def part_spec(rows, part):
        return pl.BlockSpec(
            (rows, step), lambda i: (0, jnp.clip(i - part * share, 0, share - 1))
        )

    parts = range(len(nears))
    return pl.pallas_call(
        functools.partial(blend_kernel, width**-0.5, heads, len(pieces), len(nears)),
        out_shape=(
            jax.ShapeDtypeStruct((tokens, columns), BF16),
            jax.ShapeDtypeStruct((2 * cube_count, columns), F32),
        ),
        grid=(columns // step,),
        in_specs=[smem(), smem()]
        + [piece_spec(piece, 0) for piece in pieces]
        + [piece_spec(piece, 1) for piece in pieces]
        + [part_spec(tokens, part) for part in parts]
        + [part_spec(cube_count, part) for part in parts],
        out_specs=(
            pl.BlockSpec((tokens, step), lambda i: (0, i)),
            pl.BlockSpec((2 * cube_count, step), lambda i: (0, i)),
        ),
        name="blend",
        compiler_params=pltpu.CompilerParams(vmem_limit_bytes=16 * MB),
        cost_estimate=pl.CostEstimate(
            flops=2 * tokens * columns, bytes_accessed=6 * tokens * columns, transcendentals=0
        ),
    )(gate_coarse, gate_fine, *pieces, *pieces, *nears, *pooled_queries)


def patch_kernel(
    scale,
    shift,
    info_hbm,
    tiles_hbm,
    pairs_hbm,
    sums_hbm,
    coarse_hbm,
    base_ref,
    out_ref,
    tiles_ref,
    pairs_ref,
    sums_ref,
    coarse_ref,
    ready_ref,
    info_ref,
    load_sems,
    coarse_sem,
    store_sem,
):
    dense, _, width = sums_ref.shape
    cube_count = coarse_ref.shape[0] // 2
    slots_ref, rows_ref, count_at = list_parts(info_ref, dense)
    coarse_load = pltpu.make_async_copy(coarse_hbm, coarse_ref, coarse_sem)
    info_load = pltpu.make_async_copy(info_hbm, info_ref, store_sem)
    info_load.start()

    def batch_load(step, which):
        source, target = ((pairs_hbm, pairs_ref), (sums_hbm, sums_ref))[which]
        where = pl.ds(step * PATCH_BATCH, PATCH_BATCH)
        return pltpu.make_async_copy(source.at[where], target.at[where], load_sems.at[which, step])

    def store(i):
        row = rows_ref[i]
        cube = lax.shift_right_logical(row, shift)
        head = row & ((1 << shift) - 1)
        where = (
            pl.ds(pl.multiple_of(cube * CUBE, CUBE), CUBE),
            pl.ds(pl.multiple_of(head * width, width), width),
        )
        return pltpu.make_async_copy(ready_ref.at[i], out_ref.at[where], store_sem)

    for which in range(2):
        batch_load(0, which).start()
    coarse_load.start()
    info_load.wait()
    count = info_ref[count_at]
    steps = pl.cdiv(count, PATCH_BATCH)

    @pl.loop(0, steps)
    def _(step):
        for part in range(PATCH_BATCH):
            i = step * PATCH_BATCH + part
            tile = tiles_hbm.at[slots_ref[i] - 1]
            pltpu.make_async_copy(tile, tiles_ref.at[i], load_sems.at[2, step]).start()

        @pl.when(step > 0)
        def _():
            for which in range(2):
                batch_load(step, which).start()

    for which in range(2):
        batch_load(0, which).wait()
    coarse_load.wait()

    @pl.loop(0, steps)
    def _(step):
        first = step * PATCH_BATCH
        parts = range(PATCH_BATCH)

        @pl.when(step > 0)
        def _():
            for which in range(2):
                batch_load(step, which).wait()

        tiles = tiles_ref.at[pl.ds(first, PATCH_BATCH)]
        pltpu.make_async_copy(tiles, tiles, load_sems.at[2, step]).wait()
        codes = [rows_ref[first + part] for part in parts]
        cubes = [lax.shift_right_logical(code, shift) for code in codes]
        heads = [code & ((1 << shift) - 1) for code in codes]
        columns = [pl.ds(pl.multiple_of(head * width, width), width) for head in heads]
        scores = [dot_t(pairs_ref[first + part, 0], tiles_ref[first + part, 0]) for part in parts]
        scores = [score * scale for score in scores]
        tops = [jnp.max(score, axis=1, keepdims=True) for score in scores]
        sums = [sums_ref[first + part] for part in parts]
        largest = [jnp.maximum(sums[part], tops[part]) for part in parts]
        raised = [
            jnp.exp2(scores[part] - largest[part][:, :CUBE]).astype(BF16) for part in parts
        ]
        ones = jnp.ones((CUBE, width), BF16)
        values = [jnp.concatenate([tiles_ref[first + part, 1], ones], axis=1) for part in parts]
        mixed = [dot_n(raised[part], values[part]) for part in parts]
        for part in parts:
            coarse = coarse_ref[:cube_count, columns[part]]
            gate = coarse_ref[cube_count : cube_count + 1, columns[part]]
            this_cube = lax.broadcasted_iota(I32, coarse.shape, 0) == cubes[part]
            coarse = jnp.sum(jnp.where(this_cube, coarse, 0.0), axis=0, keepdims=True)
            kept = jnp.exp2(sums[part] - largest[part])
            total = kept + mixed[part][:, width:]
            fine = pairs_ref[first + part, 1].astype(F32) * kept + mixed[part][:, :width]
            blended = coarse + gate * (fine / total)
            ready_ref[first + part] = blended.astype(BF16)
        for part in parts:
            pl.when(first + part < count)(store(first + part).start)

    @pl.loop(0, count)
    def _(i):
        store(i).wait()


def patch(info, tiles, pairs, sums, coarse, base, head_count):
    dense, _, width = sums.shape
    return pl.pallas_call(
        functools.partial(patch_kernel, width**-0.5 * LOG2E, row_bits(head_count)),
        out_shape=jax.ShapeDtypeStruct(base.shape, BF16),
        in_specs=[anywhere()] * 6,
        out_specs=anywhere(),
        scratch_shapes=[
            pltpu.VMEM((dense,) + tiles.shape[1:], BF16),
            pltpu.VMEM(pairs.shape, BF16),
            pltpu.VMEM(sums.shape, F32),
            pltpu.VMEM(coarse.shape, F32),
            pltpu.VMEM((dense, CUBE, width), BF16),
            pltpu.SMEM(info.shape, I32),
            pltpu.SemaphoreType.DMA((3, dense // PATCH_BATCH)),
            pltpu.SemaphoreType.DMA,
            pltpu.SemaphoreType.DMA,
        ],
        input_output_aliases={5: 0},
        name="patch",
        compiler_params=pltpu.CompilerParams(vmem_limit_bytes=LARGE),
        cost_estimate=pl.CostEstimate(
            flops=4 * dense * CUBE * CUBE * width,
            bytes_accessed=16 * dense * CUBE * width,
            transcendentals=dense * CUBE * CUBE,
        ),
    )(info, tiles, pairs, sums, coarse, base)


def per_device(queries, keys, values, block_lists, gate_coarse, gate_fine):
    head_count = gate_coarse.shape[0]
    width = queries.shape[1] // head_count
    cube_count = block_lists.shape[0]
    device_count = lax.axis_size("tm")
    codes, slot_of, kept = plan(block_lists, device_count)
    wanted = lax.all_to_all(codes, "tm", split_axis=0, concat_axis=0, tiled=True)
    pooled_pairs = pool(keys, values, codes)

    def exchange(array, mask):
        return lax.ppermute(array, "tm", [(i, i ^ mask) for i in range(device_count)])

    own = pooled_pairs[None]
    across = exchange(own, device_count // 2)
    masks = range(4, device_count // 2, 4)
    received = [exchange(own, mask) for mask in masks]
    tiles, after = gather_tiles(wanted, keys, values, pooled_pairs, head_count)
    tiles, across = lax.optimization_barrier((tiles, across))
    received += [exchange(across, mask) for mask in masks]
    fetched = lax.all_to_all(tiles, "tm", split_axis=0, concat_axis=0, tiled=True)
    quarter = join([own, across] + received, after=(after,))
    second = exchange(quarter, 2)
    info, pairs, sums = far_rows(slot_of, kept, queries, keys, values, quarter, device_count * CAP)
    split = head_count // 2
    near_a, pooled_a = near_attention(queries, keys, values, quarter, 0, split, width)
    half = join([quarter, second], after=(near_a, sums))
    third = exchange(half, 1)
    near_b, pooled_b = near_attention(
        queries, keys, values, half, split, head_count - split, width
    )
    base, coarse = blend(
        gate_coarse,
        gate_fine,
        [half, third],
        [near_a, near_b],
        [pooled_a, pooled_b],
        5 if split % 5 == 0 else 1,
        width,
    )
    return patch(info, fetched, pairs, sums, coarse, base, head_count)


def solution(mesh):
    return jax.shard_map(
        per_device,
        mesh=mesh,
        in_specs=(
            P(("groups", "tm"), None),
            P(("groups", "tm"), None),
            P(("groups", "tm"), None),
            P(("groups", "tm"), None, None),
            P(),
            P(),
        ),
        out_specs=P(("groups", "tm"), None),
        check_vma=False,
    )
```

```python
import functools
import math

import jax
import jax.numpy as jnp
from jax import lax
from jax.experimental import pallas as pl
from jax.experimental.pallas import tpu as pltpu
from jax.sharding import PartitionSpec as P

CUBE = 64
CAP = 4
LOG2E = math.log2(math.e)
LANES = 128
PATCH_BATCH = 15
PRE_BATCH = 5
NEAR_STEP = 256
NEAR_WEIGHT = 20
GATHER_WEIGHT = 10**12
GATHER_BATCH = 4
MB = 1024 * 1024
SMALL = 6 * MB
LARGE = 56 * MB
F32 = jnp.float32
BF16 = jnp.bfloat16
I32 = jnp.int32


def vmem():
    return pl.BlockSpec(memory_space=pltpu.VMEM)


def smem():
    return pl.BlockSpec(memory_space=pltpu.SMEM)


def anywhere():
    return pl.BlockSpec(memory_space=pl.ANY)


def dot_t(a, b):
    return lax.dot_general(a, b, (((1,), (1,)), ((), ())), preferred_element_type=F32)


def dot_n(a, b):
    return lax.dot_general(a, b, (((1,), (0,)), ((), ())), preferred_element_type=F32)


def row_bits(head_count):
    return (head_count - 1).bit_length()


def plan_kernel(lists_hbm, codes_ref, slots_ref, kept_ref, lists_ref, sem):
    lists_load = pltpu.make_async_copy(lists_hbm, lists_ref, sem)
    lists_load.start()
    me = lax.axis_index("tm")
    cube_count, list_len, head_count = lists_ref.shape
    device_count = codes_ref.shape[0]
    cube_bits = cube_count.bit_length() - 1
    shift = row_bits(head_count)
    grid = (device_count, cube_count, head_count)
    flat = (device_count * cube_count, head_count)
    owner = lax.broadcasted_iota(I32, grid, 0)
    head = lax.broadcasted_iota(I32, grid, 2)
    square = (head_count, head_count)
    before = lax.broadcasted_iota(I32, square, 0) < lax.broadcasted_iota(I32, square, 1)
    before = jnp.where(before, 1.0, 0.0).astype(BF16)
    ones = jnp.ones(square, BF16)
    block = (flat[0], flat[0])
    high = lax.broadcasted_iota(I32, block, 0)
    low = lax.broadcasted_iota(I32, block, 1)
    same = lax.shift_right_logical(high, cube_bits) == lax.shift_right_logical(low, cube_bits)
    earlier = jnp.where(same & (low < high), 1.0, 0.0).astype(BF16)
    lane = lax.broadcasted_iota(I32, (head_count, LANES), 1)
    at_slots = [jnp.where(lane == slot, 1.0, 0.0).astype(BF16) for slot in range(CAP)]
    lists_load.wait()
    lists = lists_ref[...]
    far = lax.shift_right_arithmetic(lists, cube_bits) != me
    local = lists & (cube_count - 1)
    far_value = jnp.max(jnp.where(far, lists, -1), axis=1)
    value = jnp.broadcast_to(far_value[None], grid)
    hit = jnp.where(lax.shift_right_arithmetic(value, cube_bits) == owner, 1.0, 0.0)
    hit = hit.astype(F32).reshape(flat)
    hit_b = hit.astype(BF16)
    rank = dot_n(hit_b, before)
    total = dot_n(hit_b, ones)
    rank = rank + dot_n(earlier, total.astype(BF16))
    bits = jnp.where(far, 0, lax.shift_left(jnp.ones_like(local), local))
    kept_ref[...] = jnp.sum(bits, axis=1)
    code = lax.shift_left(value & (cube_count - 1), shift) | head
    code = (code + 1).astype(F32).reshape(flat) * hit
    chosen = [jnp.where(rank == float(slot), code, 0.0).astype(BF16) for slot in range(CAP)]
    codes = sum(dot_n(chosen[slot], at_slots[slot]) for slot in range(CAP))
    codes = jnp.sum(codes.reshape(device_count, cube_count, LANES), axis=1)
    codes_ref[...] = codes.astype(I32)
    slot_of = owner.astype(F32) * CAP + rank.reshape(grid) + 1.0
    slots_ref[...] = jnp.sum(slot_of * hit.reshape(grid), axis=0).astype(I32)


def plan(block_lists, device_count):
    lists = jnp.transpose(block_lists, (0, 2, 1))
    rows = jax.ShapeDtypeStruct(block_lists.shape[:2], I32)
    return pl.pallas_call(
        plan_kernel,
        out_shape=(jax.ShapeDtypeStruct((device_count, LANES), I32), rows, rows),
        in_specs=[anywhere()],
        out_specs=(vmem(),) * 3,
        scratch_shapes=[pltpu.VMEM(lists.shape, I32), pltpu.SemaphoreType.DMA],
        name="plan",
        compiler_params=pltpu.CompilerParams(vmem_limit_bytes=LARGE),
        cost_estimate=pl.CostEstimate(flops=1000000, bytes_accessed=64 * 1024, transcendentals=0),
    )(lists)


def pool_kernel(k_hbm, v_hbm, after_ref, pooled_ref, k_ref, v_ref, sums_ref, sems):
    cubes = pooled_ref.shape[1]
    loads = {}
    for cube in range(0, cubes, 2):
        where = pl.ds(cube * CUBE, 2 * CUBE)
        for i, (source, target) in enumerate(((k_hbm, k_ref), (v_hbm, v_ref))):
            load = pltpu.make_async_copy(source.at[where], target.at[where], sems.at[i, cube])
            load.start()
            loads[i, cube] = load
    for cube in range(cubes):
        for i, target in enumerate((k_ref, v_ref)):
            if cube % 2 == 0:
                loads[i, cube].wait()
            tokens = target[cube * CUBE : (cube + 1) * CUBE, :].astype(F32)
            sums_ref[i, cube : cube + 1, :] = jnp.sum(tokens, axis=0, keepdims=True)
    for i in range(2):
        pooled_ref[i] = (sums_ref[i] * (1.0 / CUBE)).astype(BF16)


def pool(keys, values, after):
    tokens, columns = keys.shape
    cubes = tokens // CUBE
    return pl.pallas_call(
        pool_kernel,
        out_shape=jax.ShapeDtypeStruct((2, cubes, columns), BF16),
        in_specs=[anywhere()] * 3,
        out_specs=vmem(),
        scratch_shapes=[
            pltpu.VMEM((tokens, columns), BF16),
            pltpu.VMEM((tokens, columns), BF16),
            pltpu.VMEM((2, cubes, columns), F32),
            pltpu.SemaphoreType.DMA((2, cubes)),
        ],
        name="pool",
        compiler_params=pltpu.CompilerParams(vmem_limit_bytes=LARGE),
        cost_estimate=pl.CostEstimate(
            flops=2 * keys.size, bytes_accessed=4 * keys.size, transcendentals=0
        ),
    )(keys, values, after)


def gather_kernel(
    shift,
    codes_hbm,
    k_hbm,
    v_hbm,
    after_ref,
    tiles_ref,
    done_ref,
    work_ref,
    codes_ref,
    slots_ref,
    load_sems,
    store_sem,
):
    slot_count, _, rows, width = tiles_ref.shape
    codes_load = pltpu.make_async_copy(codes_hbm, codes_ref, store_sem)
    codes_load.start()
    codes_load.wait()

    def scan(peer, found):
        for rank in range(CAP):
            slot = peer * CAP + rank
            code = codes_ref[peer, rank] - 1
            slots_ref[found] = slot

            @pl.when(code >= 0)
            def _():
                cube = lax.shift_right_logical(code, shift)
                head = code & ((1 << shift) - 1)
                where = (
                    pl.ds(pl.multiple_of(cube * rows, rows), rows),
                    pl.ds(pl.multiple_of(head * width, width), width),
                )
                sem = load_sems.at[found // GATHER_BATCH]
                pltpu.make_async_copy(k_hbm.at[where], work_ref.at[slot, 0], sem).start()
                pltpu.make_async_copy(v_hbm.at[where], work_ref.at[slot, 1], sem).start()

            found = found + (code >= 0).astype(I32)
        return found

    found = lax.fori_loop(0, slot_count // CAP, scan, jnp.int32(0))
    done_ref[...] = jnp.zeros_like(done_ref)

    def store_of(i):
        slot = slots_ref[i]
        return pltpu.make_async_copy(work_ref.at[slot], tiles_ref.at[slot], store_sem)

    @pl.loop(0, pl.cdiv(found, GATHER_BATCH))
    def _(batch):
        first = batch * GATHER_BATCH
        last = jnp.minimum(first + GATHER_BATCH, found)

        @pl.loop(first, last)
        def _(i):
            both = work_ref.at[slots_ref[i]]
            pltpu.make_async_copy(both, both, load_sems.at[batch]).wait()

        @pl.loop(first, last)
        def _(i):
            store_of(i).start()

    @pl.loop(0, found)
    def _(i):
        store_of(i).wait()


def gather_tiles(codes, keys, values, after, head_count):
    tokens, columns = keys.shape
    slot_count = codes.shape[0] * CAP
    shape = (slot_count, 2, CUBE, columns // head_count)
    return pl.pallas_call(
        functools.partial(gather_kernel, row_bits(head_count)),
        out_shape=(
            jax.ShapeDtypeStruct(shape, BF16),
            jax.ShapeDtypeStruct((8, LANES), F32),
        ),
        in_specs=[anywhere()] * 4,
        out_specs=(anywhere(), vmem()),
        scratch_shapes=[
            pltpu.VMEM(shape, BF16),
            pltpu.SMEM(codes.shape, I32),
            pltpu.SMEM((slot_count + 1,), I32),
            pltpu.SemaphoreType.DMA((pl.cdiv(slot_count, GATHER_BATCH),)),
            pltpu.SemaphoreType.DMA,
        ],
        name="gather_tiles",
        compiler_params=pltpu.CompilerParams(vmem_limit_bytes=64 * MB),
        cost_estimate=pl.CostEstimate(
            flops=GATHER_WEIGHT, bytes_accessed=4 * math.prod(shape), transcendentals=0
        ),
    )(codes, keys, values, after)


def join_kernel(piece_count, *refs):
    out_ref = refs[-1]
    start = 0
    for piece in refs[:piece_count]:
        out_ref[start : start + piece.shape[0]] = piece[...]
        start += piece.shape[0]


def join(pieces, after=()):
    shape = (sum(piece.shape[0] for piece in pieces),) + pieces[0].shape[1:]
    return pl.pallas_call(
        functools.partial(join_kernel, len(pieces)),
        out_shape=jax.ShapeDtypeStruct(shape, BF16),
        in_specs=[vmem()] * len(pieces) + [anywhere()] * len(after),
        out_specs=vmem(),
        name="join",
        compiler_params=pltpu.CompilerParams(vmem_limit_bytes=SMALL),
        cost_estimate=pl.CostEstimate(
            flops=0, bytes_accessed=4 * math.prod(shape), transcendentals=0
        ),
    )(*pieces, *after)


def near_kernel(scale, q_ref, k_ref, v_ref, after_ref, out_ref, pooled_ref):
    tokens, width = q_ref.shape
    cubes = pooled_ref.shape[0]
    sums = jnp.sum(q_ref[...].astype(F32).reshape(cubes, CUBE, width), axis=1)
    pooled_ref[...] = (sums * (1.0 / CUBE)).astype(BF16)
    keys = k_ref[...]
    values = jnp.concatenate([v_ref[...], jnp.ones(v_ref.shape, BF16)], axis=1)
    step = NEAR_STEP
    starts = range(0, tokens, step)
    scores = dot_t(q_ref[0:step, :], keys)
    for start in starts:
        following = start + step
        if following < tokens:
            next_scores = dot_t(q_ref[following : following + step, :], keys)
        largest = jnp.max(scores, axis=1, keepdims=True)
        raised = jnp.exp2((scores - largest) * scale)
        mixed = dot_n(raised.astype(BF16), values)
        out_ref[start : start + step, :] = mixed[:, :width] / mixed[:, width:]
        if following < tokens:
            scores = next_scores


def near_attention(queries, keys, values, after, first, heads, width):
    tokens = queries.shape[0]
    block = pl.BlockSpec((tokens, width), lambda i: (0, first + i))
    return pl.pallas_call(
        functools.partial(near_kernel, width**-0.5 * LOG2E),
        out_shape=(
            jax.ShapeDtypeStruct((tokens, heads * width), F32),
            jax.ShapeDtypeStruct((tokens // CUBE, heads * width), BF16),
        ),
        grid=(heads,),
        in_specs=[block] * 3 + [anywhere()],
        out_specs=(
            pl.BlockSpec((tokens, width), lambda i: (0, i)),
            pl.BlockSpec((tokens // CUBE, width), lambda i: (0, i)),
        ),
        name="near_attention",
        compiler_params=pltpu.CompilerParams(vmem_limit_bytes=SMALL),
        cost_estimate=pl.CostEstimate(
            flops=NEAR_WEIGHT * 4 * tokens * tokens * heads * width,
            bytes_accessed=10 * tokens * heads * width,
            transcendentals=tokens * tokens * heads,
        ),
    )(queries, keys, values, after)


class Part:
    def __init__(self, ref, start):
        self.ref, self.start = ref, start

    def __getitem__(self, i):
        return self.ref[self.start + i]

    def __setitem__(self, i, value):
        self.ref[self.start + i] = value


def list_parts(info_ref, dense):
    return Part(info_ref, 0), Part(info_ref, dense), 2 * dense


def pre_kernel(
    scale,
    shift,
    slot_of_ref,
    kept_ref,
    q_ref,
    k_ref,
    v_ref,
    after_ref,
    info_ref,
    pairs_ref,
    sums_ref,
    sets_ref,
):
    cube_count, head_count = slot_of_ref.shape
    dense, _, width = sums_ref.shape
    tokens = q_ref.shape[0]
    slots_ref, rows_ref, count_at = list_parts(info_ref, dense)
    slots_ref[0] = 1
    rows_ref[0] = 0
    sets_ref[0] = 1

    def scan(cube, found):
        for head in range(head_count):
            slot = slot_of_ref[cube, head]
            slots_ref[found] = slot
            rows_ref[found] = lax.shift_left(cube, shift) | head
            sets_ref[found] = kept_ref[cube, head]
            found = found + (slot > 0).astype(I32)
        return found

    found = lax.fori_loop(0, cube_count, scan, jnp.int32(0))
    info_ref[count_at] = found
    last = jnp.maximum(found - 1, 0)
    for more in range(PATCH_BATCH):
        slots_ref[found + more] = slots_ref[last]
        rows_ref[found + more] = rows_ref[last]
        sets_ref[found + more] = sets_ref[last]
    cube_of = lax.broadcasted_iota(I32, (1, tokens), 1) // CUBE

    @pl.loop(0, pl.cdiv(found, PATCH_BATCH) * (PATCH_BATCH // PRE_BATCH))
    def _(step):
        first = step * PRE_BATCH
        parts = range(PRE_BATCH)
        codes = [rows_ref[first + part] for part in parts]
        cubes = [lax.shift_right_logical(code, shift) for code in codes]
        heads = [code & ((1 << shift) - 1) for code in codes]
        columns = [pl.ds(pl.multiple_of(head * width, width), width) for head in heads]
        queries = [
            q_ref[pl.ds(pl.multiple_of(cubes[part] * CUBE, CUBE), CUBE), columns[part]]
            for part in parts
        ]
        scores = [dot_t(queries[part], k_ref[:, columns[part]]) for part in parts]
        for part in parts:
            kept = (lax.shift_right_logical(sets_ref[first + part], cube_of) & 1) > 0
            scores[part] = jnp.where(kept, scores[part], -3e38)
        largest = [jnp.max(score, axis=1, keepdims=True) for score in scores]
        raised = [
            jnp.exp2((scores[part] - largest[part]) * scale).astype(BF16) for part in parts
        ]
        ones = jnp.ones((tokens, width), BF16)
        values = [jnp.concatenate([v_ref[:, columns[part]], ones], axis=1) for part in parts]
        mixed = [dot_n(raised[part], values[part]) for part in parts]
        for part in parts:
            pairs_ref[first + part, 0] = queries[part]
            total = mixed[part][:, width:]
            pairs_ref[first + part, 1] = (mixed[part][:, :width] / total).astype(BF16)
            sums_ref[first + part] = largest[part] * scale + jnp.log2(total)


def far_rows(slot_of, kept, queries, keys, values, after, slot_count):
    tokens, columns = queries.shape
    head_count = slot_of.shape[1]
    width = columns // head_count
    dense = (slot_count // PATCH_BATCH + 2) * PATCH_BATCH
    return pl.pallas_call(
        functools.partial(pre_kernel, width**-0.5 * LOG2E, row_bits(head_count)),
        out_shape=(
            jax.ShapeDtypeStruct((2 * dense + 1,), I32),
            jax.ShapeDtypeStruct((dense, 2, CUBE, width), BF16),
            jax.ShapeDtypeStruct((dense, CUBE, width), F32),
        ),
        in_specs=[smem(), smem(), vmem(), vmem(), vmem(), anywhere()],
        out_specs=(smem(), vmem(), vmem()),
        scratch_shapes=[pltpu.SMEM((dense,), I32)],
        name="far_rows",
        compiler_params=pltpu.CompilerParams(vmem_limit_bytes=SMALL),
        cost_estimate=pl.CostEstimate(
            flops=4 * slot_count * CUBE * tokens * width,
            bytes_accessed=6 * tokens * columns,
            transcendentals=slot_count * CUBE * tokens,
        ),
    )(slot_of, kept, queries, keys, values, after)


def blend_kernel(scale, heads, pieces, parts, gc_ref, gf_ref, *refs):
    key_refs, value_refs = refs[:pieces], refs[pieces : 2 * pieces]
    near_refs = refs[2 * pieces : 2 * pieces + parts]
    query_refs = refs[2 * pieces + parts : 2 * pieces + 2 * parts]
    out_ref, coarse_ref = refs[2 * pieces + 2 * parts :]
    cube_count, columns = coarse_ref.shape[0] // 2, coarse_ref.shape[1]
    width = columns // heads
    first = pl.program_id(0) * heads
    places = [slice(part * width, (part + 1) * width) for part in range(heads)]

    def gathered(piece_refs, here):
        flat = [ref[:, 0, :, here].reshape(-1, width) for ref in piece_refs]
        return jnp.concatenate(flat, axis=0)

    def put(near_ref, query_ref):
        keys = [gathered(key_refs, here) for here in places]
        values = [gathered(value_refs, here) for here in places]
        scores = [dot_t(query_ref[:, here], key) for here, key in zip(places, keys)]
        scores = jnp.concatenate(scores, axis=0) * scale
        largest = jnp.max(scores, axis=1, keepdims=True)
        raised = jnp.exp(scores - largest)
        weights = raised / jnp.sum(raised, axis=1, keepdims=True)
        coarse = []
        for part in range(heads):
            mine = weights[part * cube_count : (part + 1) * cube_count].astype(BF16)
            coarse.append(gc_ref[first + part] * dot_n(mine, values[part]))
        for part, here in enumerate(places):
            coarse_ref[:cube_count, here] = coarse[part]
            gate = jnp.full((cube_count, width), gf_ref[first + part], F32)
            coarse_ref[cube_count:, here] = gate
            near = near_ref[:, here].reshape(cube_count, CUBE, width)
            blended = coarse[part][:, None, :] + gf_ref[first + part] * near
            out_ref[:, here] = blended.reshape(cube_count * CUBE, width).astype(BF16)

    share = pl.num_programs(0) // parts
    for part in range(parts):
        chosen = functools.partial(put, near_refs[part], query_refs[part])
        pl.when(pl.program_id(0) // share == part)(chosen)


def blend(gate_coarse, gate_fine, pieces, nears, pooled_queries, heads, width):
    tokens, part_columns = nears[0].shape
    cube_count = tokens // CUBE
    columns = part_columns * len(nears)
    step = heads * width
    share = part_columns // step

    def piece_spec(piece, which):
        shape = (piece.shape[0], 1, cube_count, step)
        return pl.BlockSpec(shape, lambda i: (0, which, 0, i))

    def part_spec(rows, part):
        return pl.BlockSpec(
            (rows, step), lambda i: (0, jnp.clip(i - part * share, 0, share - 1))
        )

    parts = range(len(nears))
    return pl.pallas_call(
        functools.partial(blend_kernel, width**-0.5, heads, len(pieces), len(nears)),
        out_shape=(
            jax.ShapeDtypeStruct((tokens, columns), BF16),
            jax.ShapeDtypeStruct((2 * cube_count, columns), F32),
        ),
        grid=(columns // step,),
        in_specs=[smem(), smem()]
        + [piece_spec(piece, 0) for piece in pieces]
        + [piece_spec(piece, 1) for piece in pieces]
        + [part_spec(tokens, part) for part in parts]
        + [part_spec(cube_count, part) for part in parts],
        out_specs=(
            pl.BlockSpec((tokens, step), lambda i: (0, i)),
            pl.BlockSpec((2 * cube_count, step), lambda i: (0, i)),
        ),
        name="blend",
        compiler_params=pltpu.CompilerParams(vmem_limit_bytes=16 * MB),
        cost_estimate=pl.CostEstimate(
            flops=2 * tokens * columns, bytes_accessed=6 * tokens * columns, transcendentals=0
        ),
    )(gate_coarse, gate_fine, *pieces, *pieces, *nears, *pooled_queries)


def patch_kernel(
    scale,
    shift,
    info_hbm,
    tiles_hbm,
    pairs_hbm,
    sums_hbm,
    coarse_hbm,
    base_ref,
    out_ref,
    tiles_ref,
    pairs_ref,
    sums_ref,
    coarse_ref,
    ready_ref,
    info_ref,
    load_sems,
    coarse_sem,
    store_sem,
):
    dense, _, width = sums_ref.shape
    cube_count = coarse_ref.shape[0] // 2
    slots_ref, rows_ref, count_at = list_parts(info_ref, dense)
    coarse_load = pltpu.make_async_copy(coarse_hbm, coarse_ref, coarse_sem)
    info_load = pltpu.make_async_copy(info_hbm, info_ref, store_sem)
    info_load.start()

    def batch_load(step, which):
        source, target = ((pairs_hbm, pairs_ref), (sums_hbm, sums_ref))[which]
        where = pl.ds(step * PATCH_BATCH, PATCH_BATCH)
        return pltpu.make_async_copy(source.at[where], target.at[where], load_sems.at[which, step])

    def store(i):
        row = rows_ref[i]
        cube = lax.shift_right_logical(row, shift)
        head = row & ((1 << shift) - 1)
        where = (
            pl.ds(pl.multiple_of(cube * CUBE, CUBE), CUBE),
            pl.ds(pl.multiple_of(head * width, width), width),
        )
        return pltpu.make_async_copy(ready_ref.at[i], out_ref.at[where], store_sem)

    for which in range(2):
        batch_load(0, which).start()
    coarse_load.start()
    info_load.wait()
    count = info_ref[count_at]
    steps = pl.cdiv(count, PATCH_BATCH)

    @pl.loop(0, steps)
    def _(step):
        for part in range(PATCH_BATCH):
            i = step * PATCH_BATCH + part
            tile = tiles_hbm.at[slots_ref[i] - 1]
            pltpu.make_async_copy(tile, tiles_ref.at[i], load_sems.at[2, step]).start()

        @pl.when(step > 0)
        def _():
            for which in range(2):
                batch_load(step, which).start()

    for which in range(2):
        batch_load(0, which).wait()
    coarse_load.wait()

    @pl.loop(0, steps)
    def _(step):
        first = step * PATCH_BATCH
        parts = range(PATCH_BATCH)

        @pl.when(step > 0)
        def _():
            for which in range(2):
                batch_load(step, which).wait()

        tiles = tiles_ref.at[pl.ds(first, PATCH_BATCH)]
        pltpu.make_async_copy(tiles, tiles, load_sems.at[2, step]).wait()
        codes = [rows_ref[first + part] for part in parts]
        cubes = [lax.shift_right_logical(code, shift) for code in codes]
        heads = [code & ((1 << shift) - 1) for code in codes]
        columns = [pl.ds(pl.multiple_of(head * width, width), width) for head in heads]
        scores = [dot_t(pairs_ref[first + part, 0], tiles_ref[first + part, 0]) for part in parts]
        scores = [score * scale for score in scores]
        tops = [jnp.max(score, axis=1, keepdims=True) for score in scores]
        sums = [sums_ref[first + part] for part in parts]
        largest = [jnp.maximum(sums[part], tops[part]) for part in parts]
        raised = [
            jnp.exp2(scores[part] - largest[part][:, :CUBE]).astype(BF16) for part in parts
        ]
        ones = jnp.ones((CUBE, width), BF16)
        values = [jnp.concatenate([tiles_ref[first + part, 1], ones], axis=1) for part in parts]
        mixed = [dot_n(raised[part], values[part]) for part in parts]
        for part in parts:
            coarse = coarse_ref[:cube_count, columns[part]]
            gate = coarse_ref[cube_count : cube_count + 1, columns[part]]
            this_cube = lax.broadcasted_iota(I32, coarse.shape, 0) == cubes[part]
            coarse = jnp.sum(jnp.where(this_cube, coarse, 0.0), axis=0, keepdims=True)
            kept = jnp.exp2(sums[part] - largest[part])
            total = kept + mixed[part][:, width:]
            fine = pairs_ref[first + part, 1].astype(F32) * kept + mixed[part][:, :width]
            blended = coarse + gate * (fine / total)
            ready_ref[first + part] = blended.astype(BF16)
        for part in parts:
            pl.when(first + part < count)(store(first + part).start)

    @pl.loop(0, count)
    def _(i):
        store(i).wait()


def patch(info, tiles, pairs, sums, coarse, base, head_count):
    dense, _, width = sums.shape
    return pl.pallas_call(
        functools.partial(patch_kernel, width**-0.5 * LOG2E, row_bits(head_count)),
        out_shape=jax.ShapeDtypeStruct(base.shape, BF16),
        in_specs=[anywhere()] * 6,
        out_specs=anywhere(),
        scratch_shapes=[
            pltpu.VMEM((dense,) + tiles.shape[1:], BF16),
            pltpu.VMEM(pairs.shape, BF16),
            pltpu.VMEM(sums.shape, F32),
            pltpu.VMEM(coarse.shape, F32),
            pltpu.VMEM((dense, CUBE, width), BF16),
            pltpu.SMEM(info.shape, I32),
            pltpu.SemaphoreType.DMA((3, dense // PATCH_BATCH)),
            pltpu.SemaphoreType.DMA,
            pltpu.SemaphoreType.DMA,
        ],
        input_output_aliases={5: 0},
        name="patch",
        compiler_params=pltpu.CompilerParams(vmem_limit_bytes=LARGE),
        cost_estimate=pl.CostEstimate(
            flops=4 * dense * CUBE * CUBE * width,
            bytes_accessed=16 * dense * CUBE * width,
            transcendentals=dense * CUBE * CUBE,
        ),
    )(info, tiles, pairs, sums, coarse, base)


def per_device(queries, keys, values, block_lists, gate_coarse, gate_fine):
    head_count = gate_coarse.shape[0]
    width = queries.shape[1] // head_count
    cube_count = block_lists.shape[0]
    device_count = lax.axis_size("tm")
    codes, slot_of, kept = plan(block_lists, device_count)
    wanted = lax.all_to_all(codes, "tm", split_axis=0, concat_axis=0, tiled=True)
    pooled_pairs = pool(keys, values, codes)

    def exchange(array, mask):
        return lax.ppermute(array, "tm", [(i, i ^ mask) for i in range(device_count)])

    own = pooled_pairs[None]
    across = exchange(own, device_count // 2 + 1)
    masks = range(5, device_count // 2, 4)
    received = [exchange(own, mask) for mask in masks]
    tiles, after = gather_tiles(wanted, keys, values, pooled_pairs, head_count)
    tiles, across = lax.optimization_barrier((tiles, across))
    received += [exchange(across, mask) for mask in masks]
    fetched = lax.all_to_all(tiles, "tm", split_axis=0, concat_axis=0, tiled=True)
    quarter = join([own, across] + received, after=(after,))
    second = exchange(quarter, 2)
    info, pairs, sums = far_rows(slot_of, kept, queries, keys, values, quarter, device_count * CAP)
    split = head_count // 2
    near_a, pooled_a = near_attention(queries, keys, values, quarter, 0, split, width)
    half = join([quarter, second], after=(near_a, sums))
    third = exchange(half, 1)
    near_b, pooled_b = near_attention(
        queries, keys, values, half, split, head_count - split, width
    )
    base, coarse = blend(
        gate_coarse,
        gate_fine,
        [half, third],
        [near_a, near_b],
        [pooled_a, pooled_b],
        5 if split % 5 == 0 else 1,
        width,
    )
    return patch(info, fetched, pairs, sums, coarse, base, head_count)


def solution(mesh):
    return jax.shard_map(
        per_device,
        mesh=mesh,
        in_specs=(
            P(("groups", "tm"), None),
            P(("groups", "tm"), None),
            P(("groups", "tm"), None),
            P(("groups", "tm"), None, None),
            P(),
            P(),
        ),
        out_specs=P(("groups", "tm"), None),
        check_vma=False,
    )
```
